128 devices in a mesh: pair: 2 (over y_lo), vocab: 8 (over x, core), tok: 8 (over y_hi, z).
Axes of the slice: x: 4, y: 4 (y_hi: 2, y_lo: 2; y = y_hi * 2 + y_lo), z: 4, core: 2. Of those that a mesh axis runs over, the one named last changes fastest.
Arguments:
- teacher_hidden: bfloat16 [512, 4608], P(('pair', 'vocab', 'tok')), may hold values from -64 to 64
- teacher_gain: float32 [4608], replicated, may hold values from 0.1 to 1.9
- teacher_weight: bfloat16 [4608, 64, 2, 1024], P(None, ('vocab', 'tok'), 'pair'), may hold values from -4 to 4
- student_hidden: bfloat16 [512, 3584], P(('vocab', 'tok'), 'pair'), may hold values from -64 to 64
- student_gain: float32 [3584], P('pair'), may hold values from 0.1 to 1.9
- student_weight: bfloat16 [3584, 131072], P('pair', ('vocab', 'tok')), may hold values from -4 to 4
- token_weight: float32 [512], P('pair'), may hold values from 256 to 2048
Outputs:
- d_hidden: float32 [512, 3584], P(('vocab', 'tok'), 'pair')
- d_weight: bfloat16 [3584, 131072], P('pair', ('vocab', 'tok'))
The draws below stay inside these ranges and needn't reach their ends.
All inputs are finite; a program needn't handle non-finite values.
Results may differ from the reference program's by a relative error of at most 0.0097.
Values may be sent and summed in bfloat16 or wider, within the bound.
A program may use at most 128 MiB of HBM per device.

```python
import math
import jax
import jax.numpy as jnp
from jax import lax

DT = 4608
DS = 3584
VT_DEV = 1024
SHARDS = 64
VOCAB = 131072
TOKENS = 512


def spread_scales(key, rows, cols, low, high):
    first, second = jax.random.split(key)
    row_scale = jnp.exp(jax.random.uniform(first, (rows, 1), jnp.float32, jnp.log(low), jnp.log(high)))
    col_scale = jnp.exp(jax.random.uniform(second, (1, cols), jnp.float32, jnp.log(low), jnp.log(high)))
    return row_scale * col_scale


def column_sigma(index):
    return 3.0 + 1.5 * index.astype(jnp.float32) / VOCAB


def draw_teacher_hidden(key, part):
    key = jax.random.fold_in(key, 11)
    first, second = jax.random.split(key, 2)
    scales = spread_scales(first, TOKENS, DT, 0.3, 3.0)
    base = jnp.clip(jax.random.normal(second, (TOKENS, DT), jnp.float32), -6.0, 6.0)
    return (base * scales).astype(jnp.bfloat16)


def draw_student_hidden(key, part):
    key = jax.random.fold_in(key, 23)
    first, second = jax.random.split(key, 2)
    scales = spread_scales(first, TOKENS, DS, 0.3, 3.0)
    base = jnp.clip(jax.random.normal(second, (TOKENS, DS), jnp.float32), -6.0, 6.0)
    return (base * scales).astype(jnp.bfloat16)


def draw_teacher_weight(key, part):
    key = jax.random.fold_in(key, 37)
    shape = (DT, SHARDS, 2, VT_DEV)
    block = lax.broadcasted_iota(jnp.int32, shape, 1) * 2 + lax.broadcasted_iota(jnp.int32, shape, 2)
    index = block * VT_DEV + lax.broadcasted_iota(jnp.int32, shape, 3)
    sigma = column_sigma(index)
    base = jnp.clip(jax.random.normal(key, shape, jnp.float32), -6.0, 6.0)
    return (base * sigma / jnp.sqrt(jnp.float32(DT))).astype(jnp.bfloat16)


def draw_student_weight(key, part):
    key = jax.random.fold_in(key, 41)
    shape = (DS, VOCAB)
    index = lax.broadcasted_iota(jnp.int32, shape, 1)
    sigma = column_sigma(index)
    base = jnp.clip(jax.random.normal(key, shape, jnp.float32), -6.0, 6.0)
    return (base * sigma / jnp.sqrt(jnp.float32(DS))).astype(jnp.bfloat16)


def block_scale(key, extent, pieces, low, high):
    loudness = 1.0
    for dim, parts in pieces:
        draws = jax.random.uniform(jax.random.fold_in(jax.random.fold_in(key, 6), dim), (parts,), jnp.float32, low / len(pieces), high / len(pieces))
        loudness = loudness * jnp.repeat(jnp.exp(draws), extent[dim] // parts).reshape((-1,) + (1,) * (len(extent) - 1 - dim))
    return loudness


def setup_inputs(seed: int = 0) -> dict:
    key_list = jax.random.split(jax.random.key(seed), 8)
    teacher_hidden = draw_teacher_hidden(jax.random.fold_in(key_list[7], 71), 0)
    teacher_gain = jnp.clip(1.0 + 0.18 * jax.random.normal(key_list[1], (DT,), jnp.float32), 0.1, 1.9)
    teacher_weight = draw_teacher_weight(jax.random.fold_in(key_list[7], 71), 0)
    student_hidden = draw_student_hidden(jax.random.fold_in(key_list[7], 71), 0)
    student_gain = jnp.clip(1.0 + 0.18 * jax.random.normal(key_list[4], (DS,), jnp.float32), 0.1, 1.9)
    student_weight = draw_student_weight(jax.random.fold_in(key_list[7], 71), 0)
    token_weight = jnp.clip(jnp.exp(math.log(2048.0) - 2.0794415 * jax.random.uniform(key_list[6], (TOKENS,), jnp.float32) ** block_scale(key_list[6], (TOKENS,), ((0, 2),), -0.2, 0.2)), 256.0, 2048.0)
    return dict(teacher_hidden=teacher_hidden, teacher_gain=teacher_gain, teacher_weight=teacher_weight, student_hidden=student_hidden, student_gain=student_gain, student_weight=student_weight, token_weight=token_weight)


EPS = 1e-06
CAP = 30.0

def softcap(values):
    return CAP * jnp.tanh(values / CAP)

def reference(teacher_hidden, teacher_gain, teacher_weight, student_hidden, student_gain, student_weight, token_weight):
    width_t = teacher_hidden.shape[1]
    width_s = student_hidden.shape[1]
    teach_x = teacher_hidden.astype(jnp.float32)
    teach_r = lax.rsqrt(lax.optimization_barrier(jnp.mean(teach_x * teach_x, axis=-1, keepdims=True)) + EPS)
    teach_n = (teach_x * teach_r * teacher_gain).astype(jnp.bfloat16)
    teach_w = teacher_weight.reshape(width_t, VOCAB)
    stud_x = student_hidden.astype(jnp.float32)
    stud_r = lax.rsqrt(lax.optimization_barrier(jnp.mean(stud_x * stud_x, axis=-1, keepdims=True)) + EPS)
    stud_n = (stud_x * stud_r * student_gain).astype(jnp.bfloat16)
    block = TOKENS // 8

    def one_block(index):
        start = (index * block).astype(jnp.int32)
        rows_t = lax.dynamic_slice_in_dim(teach_n, start, block, 0)
        rows_s = lax.dynamic_slice_in_dim(stud_n, start, block, 0)
        weights = lax.dynamic_slice_in_dim(token_weight, start, block, 0)
        teach_z = softcap(jnp.dot(rows_t, teach_w, preferred_element_type=jnp.float32))
        teach_e = jnp.exp(teach_z)
        probs = (teach_e / lax.optimization_barrier(jnp.sum(teach_e, axis=-1, keepdims=True))).astype(jnp.bfloat16)
        stud_z = softcap(jnp.dot(rows_s, student_weight, preferred_element_type=jnp.float32))
        stud_e = jnp.exp(stud_z)
        stud_p = stud_e / lax.optimization_barrier(jnp.sum(stud_e, axis=-1, keepdims=True))
        slope = 1.0 - (stud_z / CAP) ** 2
        return (weights[:, None] * (stud_p - probs.astype(jnp.float32)) * slope).astype(jnp.bfloat16)
    grads = lax.map(one_block, jnp.arange(8, dtype=jnp.int32)).reshape(TOKENS, VOCAB)
    d_weight = jnp.dot(stud_n.T, grads, preferred_element_type=jnp.float32).astype(jnp.bfloat16)
    d_normed = jnp.dot(grads, student_weight.T, preferred_element_type=jnp.float32)
    scaled = student_gain * d_normed
    inner = lax.optimization_barrier(jnp.sum(stud_x * scaled, axis=-1, keepdims=True))
    d_hidden = stud_r * scaled - stud_x * stud_r ** 3 * inner / width_s
    return (d_hidden, d_weight)
```

```python
import jax
import jax.numpy as jnp
from jax import lax
from jax.experimental import pallas as pl
from jax.experimental.pallas import tpu as pltpu
from jax.sharding import PartitionSpec as P

DT = 4608
DS = 3584
HS = DS // 2
CS = HS // 2
VT = 1024
EPS = 1e-06
CAP = 30.0
KT = DT // 4
MESH = pl.DeviceIdType.MESH

SLOPE = 3.0
KNEE = 64.0
LOGK = 7.2
BIAS = 125.0
LOG2E = 1.4426950408889634


def encode(b):
    a = jnp.abs(b)
    far = SLOPE * KNEE + LOGK * LOG2E * jnp.log(jnp.maximum(a, KNEE) / KNEE)
    w = jnp.where(a <= KNEE, SLOPE * a, jnp.minimum(far, 251.5)) - BIAS
    y = jnp.exp2(w)
    return jnp.where(b < 0, -y, y).astype(jnp.bfloat16)


def decode(code):
    y = code.astype(jnp.float32)
    w = jnp.log(jnp.abs(y)) * LOG2E + BIAS
    a = jnp.where(
        w <= SLOPE * KNEE,
        jnp.maximum(w, 0.0) * (1.0 / SLOPE),
        KNEE * jnp.exp2((w - SLOPE * KNEE) * (1.0 / LOGK)),
    )
    return jnp.where(y < 0, -a, a)


def row_sums(e):
    part = e[:, :128]
    for n in range(1, e.shape[1] // 128):
        part = part + e[:, n * 128 : (n + 1) * 128]
    return jnp.sum(part.T, axis=0, keepdims=True)


def column(row):
    return jnp.broadcast_to(row, (128, 128)).T


def head_kernel(
    th, tg, sh, sg, tw, wt_hbm, ws_hbm,
    dh_out, s_out, g_out,
    wt, ws, tsc, tb, tn, sq, nf, stile, s_all, zs, zr, zo, slope, et, g_all, tw2,
    ar_s, ar_r, ar2, ar3, dacc, rsib_s, rsib_r, rs_s, rs_r, fin_s, fin, inn,
    ssem, rsem, lsem,
):
    p = lax.axis_index("pair")
    v = lax.axis_index("vocab")
    t = lax.axis_index("tok")
    x, c, h, z = v // 2, lax.rem(v, 2), t // 4, lax.rem(t, 4)
    y = 2 * h + p

    def dev(p_, x_, c_, h_, z_):
        return (p_, 2 * x_ + c_, 4 * h_ + z_)

    partner = dev(1 - p, x, c, h, z)
    sibling = dev(p, x, 1 - c, h, z)

    def xdev(d):
        return dev(p, lax.rem(x + d, 4), c, h, z)

    def zdev(d):
        return dev(p, x, c, h, lax.rem(z + d, 4))

    def ydev(d):
        y_ = lax.rem(y + d, 4)
        return dev(lax.rem(y_, 2), x, c, y_ // 2, z)

    def plane_dev(k):
        return lax.rem(x + k, 4), lax.rem(z + k // 4, 4), lax.rem(h + k // 16, 2)

    def flat_dev(k):
        x_, z_, h_ = plane_dev(k)
        return dev(p, x_, c, h_, z_)

    counter = [0]
    sends = []

    def rcopy(src, dst, device):
        i = counter[0]
        counter[0] += 1
        cp = pltpu.make_async_remote_copy(
            src_ref=src, dst_ref=dst, send_sem=ssem.at[i], recv_sem=rsem.at[i],
            device_id=device, device_id_type=MESH,
        )
        cp.start()
        sends.append(cp)
        return cp

    def rwait(region, sem):
        pltpu.make_async_remote_copy(
            src_ref=region, dst_ref=region, send_sem=sem, recv_sem=sem,
            device_id=partner, device_id_type=MESH,
        ).wait_recv()

    w_cp = [
        pltpu.make_async_copy(ws_hbm.at[:, pl.ds(pl.multiple_of((1 - p) * VT, VT), VT)], ws.at[1], lsem.at[0]),
        pltpu.make_async_copy(ws_hbm.at[:, pl.ds(pl.multiple_of(p * VT, VT), VT)], ws.at[0], lsem.at[1]),
        pltpu.make_async_copy(wt_hbm, wt, lsem.at[2]),
    ]
    for cp in w_cp:
        cp.start()

    bar = pltpu.get_barrier_semaphore()
    for d in (sibling, partner, ydev(3 - 2 * p)):
        pl.semaphore_signal(bar, inc=1, device_id=d, device_id_type=MESH)

    @pl.loop(1, 32)
    def _(k):
        pl.semaphore_signal(bar, inc=1, device_id=flat_dev(k), device_id_type=MESH)

    sx = sh[...].astype(jnp.float32)
    sq[0] = jnp.broadcast_to(jnp.sum(sx * sx, axis=-1, keepdims=True), (8, 128))
    tx = th[...].astype(jnp.float32)
    tnorm = tx * lax.rsqrt(jnp.mean(tx * tx, axis=-1, keepdims=True) + EPS) * tg[...]
    for j in range(4):
        tsc[4 * j : 4 * j + 4, :] = tnorm[:, j * KT : (j + 1) * KT]
    tb[c, y, x, z] = tsc[...].astype(jnp.bfloat16)
    tw2[p] = tw[...]

    pl.semaphore_wait(bar, 34)

    sq_cp = rcopy(sq.at[0], sq.at[1], partner)
    tw_cp = rcopy(tw2.at[p], tw2.at[p], partner)
    own_t = tb.at[c, y, x, z]
    t1 = [rcopy(own_t, own_t, ydev(d)) for d in (1, 2, 3)]

    sq_cp.wait_recv()
    stud_r = lax.rsqrt((sq[0] + sq[1])[:, :1] / DS + EPS)
    snorm = sx * stud_r * sg[...]
    nf[0] = snorm[:, :CS]
    nf[1] = snorm[:, CS:]
    mine = stile.at[pl.ds(pl.multiple_of(c * 8, 8), 8)]
    n_cp = rcopy(nf.at[1 - c], mine, sibling)
    mine[...] = nf[c]
    n_cp.wait_recv()
    ccol = pl.ds(pl.multiple_of(c * CS, 128), CS)
    srows = pl.ds(pl.multiple_of(h * 256 + x * 64 + z * 16, 16), 16)
    s_all[srows, ccol] = stile[...].astype(jnp.bfloat16)
    own_s = s_all.at[srows, ccol]
    s_sem = counter[0]
    counter[0] += 2

    def s_send(k):
        return pltpu.make_async_remote_copy(
            src_ref=own_s, dst_ref=own_s, send_sem=ssem.at[s_sem], recv_sem=rsem.at[s_sem + h],
            device_id=flat_dev(k), device_id_type=MESH,
        )

    @pl.loop(1, 32)
    def _(k):
        s_send(k).start()

    for cp in t1:
        cp.wait_recv()
    t2 = [rcopy(tb.at[c, pl.ds(0, 2), x, z], tb.at[c, pl.ds(0, 2), x, z], xdev(d)) for d in (1, 2, 3)]
    t2 += [rcopy(tb.at[c, pl.ds(2, 2), x, z], tb.at[c, pl.ds(2, 2), x, z], zdev(d)) for d in (1, 2, 3)]
    for cp in w_cp:
        cp.wait()

    sib_s = []
    for k in range(2):
        @pl.when(h == k)
        def _():
            rwait(s_all.at[pl.ds(k * 256, 240), ccol], rsem.at[s_sem + k])

        @pl.when(h != k)
        def _():
            rwait(s_all.at[pl.ds(k * 256, 256), ccol], rsem.at[s_sem + k])

        region = s_all.at[pl.ds(k * 256, 256), ccol]
        sib_s.append(rcopy(region, region, sibling))
        if k == 0:
            for cp in t2:
                cp.wait_recv()
            t3 = []
            for d in (1, 2, 3):
                a = tb.at[c, pl.ds(0, 2), :, z]
                t3.append(rcopy(a, a, zdev(d)))
                b = tb.at[c, pl.ds(2, 2), x]
                t3.append(rcopy(b, b, xdev(d)))
            sib_t = []
            for r in (tb.at[c, pl.ds(0, 2), :, z], tb.at[c, pl.ds(2, 2), x]):
                sib_t.append(rcopy(r, r, sibling))

    z_cp = []
    for k in range(2):
        sib_s[k].wait_recv()
        rows = pl.ds(k * 256, 256)

        @pl.loop(0, 4)
        def _(n):
            cols = pl.ds(pl.multiple_of(n * 256, 256), 256)
            zs[rows, cols] = encode(jnp.dot(s_all[rows, :], ws[1, :, cols], preferred_element_type=jnp.float32))

        z_cp.append(rcopy(zs.at[rows], zr.at[rows], partner))
    s_cp = pltpu.make_async_copy(s_all, s_out, lsem.at[3])
    s_cp.start()

    @pl.loop(0, 4)
    def _(n):
        cols = pl.ds(pl.multiple_of(n * 256, 256), 256)
        zo[:, cols] = jnp.dot(s_all[...], ws[0, :, cols], preferred_element_type=jnp.float32)

    for i, d in enumerate((1, 2, 3)):
        z_, x_ = lax.rem(z - d + 4, 4), lax.rem(x - d + 4, 4)
        t3[2 * i].wait_recv()
        r = tb.at[c, pl.ds(0, 2), :, z_]
        sib_t.append(rcopy(r, r, sibling))
        t3[2 * i + 1].wait_recv()
        r = tb.at[c, pl.ds(2, 2), x_]
        sib_t.append(rcopy(r, r, sibling))
    for cp in sib_t:
        cp.wait_recv()

    o = lax.broadcasted_iota(jnp.int32, (256, 256), 0)
    src = lax.broadcasted_iota(jnp.int32, (256, 256), 1)
    o_j, o_r = o // 64, lax.rem(o, 4)
    o_h, o_z = lax.rem(o // 32, 2), lax.rem(o // 16, 2) * 2 + lax.rem(o // 4, 2)
    o_x = lax.rem(o // 8, 2)
    perm = (src == o_h * 128 + o_x * 64 + o_z * 16 + o_j * 4 + o_r).astype(jnp.bfloat16)

    @pl.loop(0, 8)
    def _(g):
        c_, p_, x_ = g // 4, lax.rem(g // 2, 2), lax.rem(g, 2)
        pieces = [tb[c_, 2 * a + p_, 2 * x_ + b].reshape(64, KT) for a in range(2) for b in range(2)]
        out = jnp.dot(perm, jnp.concatenate(pieces, axis=0), preferred_element_type=jnp.float32)
        out = out.astype(jnp.bfloat16)
        for j in range(4):
            tn[pl.ds(pl.multiple_of(g * 64, 64), 64), j * KT : (j + 1) * KT] = out[j * 64 : (j + 1) * 64]

    @pl.loop(0, 4)
    def _(n):
        cols = pl.ds(pl.multiple_of(n * 256, 256), 256)
        logits = jnp.dot(tn[...], wt[:, cols], preferred_element_type=jnp.float32)
        et[:, cols] = jnp.exp(CAP * jnp.tanh(logits / CAP))

    tw_cp.wait_recv()
    ar_sem = counter[0]
    counter[0] += 2
    slot = h * 16 + x * 4 + z

    def ar_send(k, i):
        return pltpu.make_async_remote_copy(
            src_ref=ar_s.at[k], dst_ref=ar_r.at[k, slot], send_sem=ssem.at[ar_sem + k], recv_sem=rsem.at[ar_sem + k],
            device_id=flat_dev(i), device_id_type=MESH,
        )

    g_cp = []
    gcol = pl.ds(pl.multiple_of(p * VT, VT), VT)
    ocol = pl.ds(pl.multiple_of((1 - p) * VT, VT), VT)
    for k in range(2):
        z_cp[k].wait_recv()
        for i in range(2):
            rows = pl.ds(k * 256 + i * 128, 128)

            @pl.loop(0, 8)
            def _(n):
                cols = pl.ds(pl.multiple_of(n * 128, 128), 128)
                th_ = jnp.tanh((zo[rows, cols] + decode(zr[rows, cols])) / CAP)
                zo[rows, cols] = jnp.exp(CAP * th_)
                slope[rows, cols] = 1.0 - th_ * th_

            ar_s[k, i : i + 1, :] = row_sums(zo[rows, :])
            ar_s[k, 2 + i : 3 + i, :] = row_sums(et[rows, :])
        ar_s[k, 4:8, :] = jnp.zeros((4, 128), jnp.float32)

        @pl.loop(1, 32)
        def _(i):
            ar_send(k, i).start()

        rwait(ar_r.at[k, pl.ds(0, 31)], rsem.at[ar_sem + k])
        ar_r[k, slot] = ar_s[k]
        ar2[k, 0] = jnp.sum(ar_r[k], axis=0)
        rcopy(ar2.at[k, 0], ar2.at[k, 1], sibling).wait_recv()
        ar3[k, 0] = ar2[k, 0] + ar2[k, 1]
        rcopy(ar3.at[k, 0], ar3.at[k, 1], partner).wait_recv()
        total = ar3[k, 0] + ar3[k, 1]
        for i in range(2):
            rows = pl.ds(k * 256 + i * 128, 128)
            w_col = column(tw2[i, k : k + 1, :])
            s_col = 1.0 / column(total[i : i + 1, :])
            t_col = 1.0 / column(total[2 + i : 3 + i, :])

            @pl.loop(0, 8)
            def _(n):
                cols = pl.ds(pl.multiple_of(n * 128, 128), 128)
                probs = (et[rows, cols] * t_col).astype(jnp.bfloat16).astype(jnp.float32)
                grad = w_col * (zo[rows, cols] * s_col - probs) * slope[rows, cols]
                g_all[rows, pl.ds(pl.multiple_of(p * VT + n * 128, 128), 128)] = grad.astype(jnp.bfloat16)

        region = g_all.at[pl.ds(k * 256, 256), gcol]
        g_cp.append(rcopy(region, region, partner))

    nt = (((1,), (1,)), ((), ()))

    @pl.loop(0, 7)
    def _(n):
        w_rows = pl.ds(pl.multiple_of(n * 256, 256), 256)
        dacc[:, w_rows] = lax.dot_general(g_all[:, gcol], ws[0, w_rows, :], nt, preferred_element_type=jnp.float32)

    rs_sem = counter[0]
    counter[0] += 3

    def rs_send(k, i):
        x_, z_ = lax.rem(x + i, 4), lax.rem(z + i // 4, 4)
        return pltpu.make_async_remote_copy(
            src_ref=rs_s.at[k, x_, z_], dst_ref=rs_r.at[slot], send_sem=ssem.at[rs_sem + k], recv_sem=rsem.at[rs_sem + 2],
            device_id=dev(p, x_, c, k, z_), device_id_type=MESH,
        )

    xcol = pl.ds(pl.multiple_of((1 - c) * CS, 128), CS)
    for k in range(2):
        rows = pl.ds(k * 256, 256)
        g_cp[k].wait_recv()

        @pl.loop(0, 7)
        def _(n):
            w_rows = pl.ds(pl.multiple_of(n * 256, 256), 256)
            dacc[rows, w_rows] += lax.dot_general(
                g_all[rows, ocol], ws[1, w_rows, :], nt, preferred_element_type=jnp.float32
            )

        rsib_s[rows, :] = dacc[rows, xcol].astype(jnp.bfloat16)
        rcopy(rsib_s.at[rows], rsib_r.at[rows], sibling).wait_recv()
        both = (dacc[rows, ccol] + rsib_r[rows, :].astype(jnp.float32)).astype(jnp.bfloat16)
        rs_s[k] = both.reshape(4, 4, 16, CS)
        first = jnp.where(h == k, 1, 0)

        @pl.loop(first, 16)
        def _(i):
            rs_send(k, i).start()

    g_out_cp = pltpu.make_async_copy(g_all, g_out, lsem.at[4])
    g_out_cp.start()

    rwait(rs_r.at[pl.ds(0, 31)], rsem.at[rs_sem + 2])
    rs_r[slot] = rs_s[h, x, z]
    done = jnp.sum(rs_r[...].astype(jnp.float32), axis=0)
    fin_s[...] = done
    fin[c] = fin_s[pl.ds(pl.multiple_of(c * 8, 8), 8)]
    rcopy(fin_s.at[pl.ds(pl.multiple_of((1 - c) * 8, 8), 8)], fin.at[c], sibling).wait_recv()
    scaled = jnp.concatenate([fin[0], fin[1]], axis=-1) * sg[...]
    inn[0] = jnp.broadcast_to(jnp.sum(sx * scaled, axis=-1, keepdims=True), (8, 128))
    rcopy(inn.at[0], inn.at[1], partner).wait_recv()
    inner = (inn[0] + inn[1])[:, :1]
    dh_out[...] = stud_r * scaled - sx * (stud_r * stud_r * stud_r) * inner / DS

    for cp in sends:
        cp.wait_send()

    @pl.loop(1, 32)
    def _(k):
        s_send(k).wait_send()
        ar_send(0, k).wait_send()
        ar_send(1, k).wait_send()

    for k in range(2):
        first = jnp.where(h == k, 1, 0)

        @pl.loop(first, 16)
        def _(i):
            rs_send(k, i).wait_send()

    s_cp.wait()
    g_out_cp.wait()


def head(th, tg, sh, sg, tw, wt, ws):
    f32, bf16 = jnp.float32, jnp.bfloat16
    vmem = pl.BlockSpec(memory_space=pltpu.VMEM)
    hbm = pl.BlockSpec(memory_space=pl.ANY)
    scratch = [
        pltpu.VMEM((DT, VT), bf16),
        pltpu.VMEM((2, HS, VT), bf16),
        pltpu.VMEM((16, KT), f32),
        pltpu.VMEM((2, 4, 4, 4, 16, KT), bf16),
        pltpu.VMEM((512, DT), bf16),
        pltpu.VMEM((2, 8, 128), f32),
        pltpu.VMEM((2, 8, CS), f32),
        pltpu.VMEM((16, CS), f32),
        pltpu.VMEM((512, HS), bf16),
        pltpu.VMEM((512, VT), bf16),
        pltpu.VMEM((512, VT), bf16),
        pltpu.VMEM((512, VT), f32),
        pltpu.VMEM((512, VT), f32),
        pltpu.VMEM((512, VT), f32),
        pltpu.VMEM((512, 2 * VT), bf16),
        pltpu.VMEM((2, 8, 128), f32),
        pltpu.VMEM((2, 8, 128), f32),
        pltpu.VMEM((2, 32, 8, 128), f32),
        pltpu.VMEM((2, 2, 8, 128), f32),
        pltpu.VMEM((2, 2, 8, 128), f32),
        pltpu.VMEM((512, HS), f32),
        pltpu.VMEM((512, CS), bf16),
        pltpu.VMEM((512, CS), bf16),
        pltpu.VMEM((2, 4, 4, 16, CS), bf16),
        pltpu.VMEM((32, 16, CS), bf16),
        pltpu.VMEM((16, CS), f32),
        pltpu.VMEM((2, 8, CS), f32),
        pltpu.VMEM((2, 8, 128), f32),
        pltpu.SemaphoreType.DMA((64,)),
        pltpu.SemaphoreType.DMA((64,)),
        pltpu.SemaphoreType.DMA((5,)),
    ]
    return pl.pallas_call(
        head_kernel,
        out_shape=(
            jax.ShapeDtypeStruct((8, HS), f32),
            jax.ShapeDtypeStruct((512, HS), bf16),
            jax.ShapeDtypeStruct((512, 2 * VT), bf16),
        ),
        in_specs=[vmem] * 5 + [hbm] * 2,
        out_specs=(vmem, hbm, hbm),
        scratch_shapes=scratch,
        compiler_params=pltpu.CompilerParams(
            collective_id=0, has_side_effects=True, vmem_limit_bytes=58 * 1024 * 1024
        ),
        name="head",
    )(th, tg, sh, sg, tw, wt, ws)


def per_device(
    teacher_hidden,
    teacher_gain,
    teacher_weight,
    student_hidden,
    student_gain,
    student_weight,
    token_weight,
):
    tw = token_weight.reshape(2, 2, 2, 4, 8).transpose(2, 0, 3, 1, 4).reshape(2, 128)
    tw = jnp.pad(tw, ((0, 6), (0, 0)))
    d_hidden, s_all, g_all = head(
        teacher_hidden,
        teacher_gain.reshape(1, DT),
        student_hidden,
        student_gain.reshape(1, HS),
        tw,
        teacher_weight.reshape(DT, VT),
        student_weight,
    )
    d_weight = lax.dot_general(
        s_all, g_all, (((0,), (0,)), ((), ())), preferred_element_type=jnp.float32
    ).astype(jnp.bfloat16)
    return (d_hidden, d_weight)


def solution(mesh):
    return jax.shard_map(
        per_device,
        mesh=mesh,
        in_specs=(
            P(("pair", "vocab", "tok"), None),
            P(),
            P(None, ("vocab", "tok"), "pair", None),
            P(("vocab", "tok"), "pair"),
            P("pair"),
            P("pair", ("vocab", "tok")),
            P("pair"),
        ),
        out_specs=(P(("vocab", "tok"), "pair"), P("pair", ("vocab", "tok"))),
        check_vma=False,
    )
```

```python
import jax
import jax.numpy as jnp
from jax import lax
from jax.experimental import pallas as pl
from jax.experimental.pallas import tpu as pltpu
from jax.sharding import PartitionSpec as P

DT = 4608
DS = 3584
HS = DS // 2
CS = HS // 2
VT = 1024
EPS = 1e-06
CAP = 30.0
KT = DT // 4
MESH = pl.DeviceIdType.MESH

SLOPE = 3.0
KNEE = 64.0
LOGK = 7.2
BIAS = 125.0
LOG2E = 1.4426950408889634


def encode(b):
    a = jnp.abs(b)
    far = SLOPE * KNEE + LOGK * LOG2E * jnp.log(jnp.maximum(a, KNEE) / KNEE)
    w = jnp.where(a <= KNEE, SLOPE * a, jnp.minimum(far, 251.5)) - BIAS
    y = jnp.exp2(w)
    return jnp.where(b < 0, -y, y).astype(jnp.bfloat16)


def decode(code):
    y = code.astype(jnp.float32)
    w = jnp.log(jnp.abs(y)) * LOG2E + BIAS
    a = jnp.where(
        w <= SLOPE * KNEE,
        jnp.maximum(w, 0.0) * (1.0 / SLOPE),
        KNEE * jnp.exp2((w - SLOPE * KNEE) * (1.0 / LOGK)),
    )
    return jnp.where(y < 0, -a, a)


def row_sums(e):
    part = e[:, :128]
    for n in range(1, e.shape[1] // 128):
        part = part + e[:, n * 128 : (n + 1) * 128]
    return jnp.sum(part.T, axis=0, keepdims=True)


def column(row):
    return jnp.broadcast_to(row, (128, 128)).T


def head_kernel(
    th, tg, sh, sg, tw, wt_hbm, ws_hbm,
    dh_out, s_out, g_out,
    wt, ws, tsc, tb, tn, sq, nf, stile, s_all, st, zs, zr, zo, slope, et, g_all, tw2,
    ar_s, ar_c, ar_r, ar_y, dacc, rsib_s, rsib_r, rs_s, rs_r, fin_s, fin, inn,
    ssem, rsem, lsem,
):
    p = lax.axis_index("pair")
    v = lax.axis_index("vocab")
    t = lax.axis_index("tok")
    x, c, h, z = v // 2, lax.rem(v, 2), t // 4, lax.rem(t, 4)
    y = 2 * h + p

    def dev(p_, x_, c_, h_, z_):
        return (p_, 2 * x_ + c_, 4 * h_ + z_)

    partner = dev(1 - p, x, c, h, z)
    sibling = dev(p, x, 1 - c, h, z)
    xs = [x] + [lax.rem(x + d, 4) for d in (1, 2, 3)]
    zs_ = [z] + [lax.rem(z + d, 4) for d in (1, 2, 3)]
    xdev = [dev(p, xs[d], c, h, z) for d in range(4)]
    zdev = [dev(p, x, c, h, zs_[d]) for d in range(4)]
    ys = [y] + [lax.rem(y + d, 4) for d in (1, 2, 3)]
    ydev = [dev(lax.rem(ys[d], 2), x, c, ys[d] // 2, z) for d in range(4)]
    hdev = ydev[2]
    cross = dev(p, x, 1 - c, 1 - h, z)
    plane = [(a, b) for b in range(4) for a in range(4)]

    counter = [0]
    sends = []
    ends = []

    class Copy:
        def __init__(self, i, src, dst, device):
            self.cp = pltpu.make_async_remote_copy(
                src_ref=src, dst_ref=dst, send_sem=ssem.at[i], recv_sem=rsem.at[i],
                device_id=device, device_id_type=MESH,
            )
            self.cp.start()
            self.here = False

        def wait_recv(self):
            if not self.here:
                self.cp.wait_recv()
            self.here = True

    def rcopy(src, dst, device):
        i = counter[0]
        counter[0] += 1
        sends.append(Copy(i, src, dst, device))
        return sends[-1]

    def finish():
        for cp in sends:
            cp.wait_recv()
            cp.cp.wait_send()
        for end in ends:
            end()

    def rwait(region, sem):
        pltpu.make_async_remote_copy(
            src_ref=region, dst_ref=region, send_sem=sem, recv_sem=sem,
            device_id=partner, device_id_type=MESH,
        ).wait_recv()

    w_cp = [
        pltpu.make_async_copy(ws_hbm.at[:, pl.ds(pl.multiple_of((1 - p) * VT, VT), VT)], ws.at[1], lsem.at[0]),
        pltpu.make_async_copy(ws_hbm.at[:, pl.ds(pl.multiple_of(p * VT, VT), VT)], ws.at[0], lsem.at[1]),
        pltpu.make_async_copy(wt_hbm, wt, lsem.at[2]),
    ]
    for cp in w_cp:
        cp.start()
    w_here = []

    def w_wait():
        if not w_here:
            for cp in w_cp:
                cp.wait()
        w_here.append(True)

    ends.append(w_wait)

    bar = pltpu.get_barrier_semaphore()
    for d in [sibling, ydev[1], ydev[2], ydev[3], cross]:
        pl.semaphore_signal(bar, inc=1, device_id=d, device_id_type=MESH)
    for a, b in plane[1:]:
        pl.semaphore_signal(bar, inc=1, device_id=dev(p, xs[a], c, h, zs_[b]), device_id_type=MESH)

    sx = sh[...].astype(jnp.float32)
    sq[0] = jnp.broadcast_to(jnp.sum(sx * sx, axis=-1, keepdims=True), (8, 128))
    tx = th[...].astype(jnp.float32)
    tnorm = tx * lax.rsqrt(jnp.mean(tx * tx, axis=-1, keepdims=True) + EPS) * tg[...].reshape(1, DT)
    for j in range(4):
        tsc[4 * j : 4 * j + 4, :] = tnorm[:, j * KT : (j + 1) * KT]
    tb[c, y, x, z] = tsc[...].astype(jnp.bfloat16)
    for b in range(2):
        tw2[p, b] = jnp.broadcast_to(tw[pl.ds(128 * b, 128)].reshape(1, 128), (8, 128))

    pl.semaphore_wait(bar, 20)

    sq_cp = rcopy(sq.at[0], sq.at[1], partner)
    tw_cp = rcopy(tw2.at[p], tw2.at[p], partner)
    own_t = tb.at[c, y, x, z]
    t1 = [rcopy(own_t, own_t, ydev[d]) for d in (1, 2, 3)]

    sq_cp.wait_recv()
    stud_r = lax.rsqrt((sq[0] + sq[1])[:, :1] / DS + EPS)
    gain = sg[...].reshape(1, HS)
    snorm = sx * stud_r * gain
    nf[0] = snorm[:, :CS]
    nf[1] = snorm[:, CS:]
    mine = stile.at[pl.ds(pl.multiple_of(c * 8, 8), 8)]
    n_cp = rcopy(nf.at[1 - c], mine, sibling)
    mine[...] = nf[c]
    n_cp.wait_recv()
    ccol = pl.ds(pl.multiple_of(c * CS, 128), CS)
    s_all[h, x, z, :, ccol] = stile[...].astype(jnp.bfloat16)
    own_s = s_all.at[h, x, z, :, ccol]
    h_cp = rcopy(own_s, own_s, hdev)
    h_cp.wait_recv()
    s2 = []
    for d in (1, 2, 3):
        a, b = s_all.at[0, x, z, :, ccol], s_all.at[1, x, z, :, ccol]
        s2.append(rcopy(a, a, xdev[d]))
        s2.append(rcopy(b, b, zdev[d]))
    for cp in t1:
        cp.wait_recv()
    t2 = []
    for d in (1, 2, 3):
        a, b = tb.at[c, pl.ds(0, 2), x, z], tb.at[c, pl.ds(2, 2), x, z]
        t2.append(rcopy(a, a, xdev[d]))
        t2.append(rcopy(b, b, zdev[d]))
    for cp in s2:
        cp.wait_recv()
    s3 = []
    for d in (1, 2, 3):
        a, b = s_all.at[0, :, z, :, ccol], s_all.at[1, x, :, :, ccol]
        s3.append(rcopy(a, a, zdev[d]))
        s3.append(rcopy(b, b, xdev[d]))
    for cp in t2:
        cp.wait_recv()
    t3 = []
    for d in (1, 2, 3):
        a, b = tb.at[c, pl.ds(0, 2), :, z], tb.at[c, pl.ds(2, 2), x]
        t3.append(rcopy(a, a, zdev[d]))
        t3.append(rcopy(b, b, xdev[d]))
    sib_t = []
    for r in (tb.at[c, pl.ds(0, 2), :, z], tb.at[c, pl.ds(2, 2), x]):
        sib_t.append(rcopy(r, r, sibling))
    sib_s = ([], [])
    for i in range(4):
        if i:
            s3[2 * i - 2].wait_recv()
        r = s_all.at[0, :, zs_[(4 - i) % 4], :, ccol]
        sib_s[0].append(rcopy(r, r, sibling))
    for i in range(4):
        if i:
            s3[2 * i - 1].wait_recv()
        r = s_all.at[1, xs[(4 - i) % 4], :, :, ccol]
        sib_s[1].append(rcopy(r, r, sibling))
    w_wait()

    z_cp = ([], [])
    for k in range(2):
        for cp in sib_s[k]:
            cp.wait_recv()
        rows = pl.ds(k * 256, 256)
        lhs = s_all[k].reshape(256, HS)
        for n in range(4):
            cols = pl.ds(n * 256, 256)
            zs[rows, cols] = encode(jnp.dot(lhs, ws[1, :, cols], preferred_element_type=jnp.float32))
            z_cp[k].append(rcopy(zs.at[rows, cols], zr.at[rows, cols], partner))


    def own_logits(k):
        rows = pl.ds(k * 256, 256)

        @pl.loop(0, 4)
        def _(n):
            cols = pl.ds(pl.multiple_of(n * 256, 256), 256)
            zo[rows, cols] = jnp.dot(s_all[k].reshape(256, HS), ws[0, :, cols], preferred_element_type=jnp.float32)

    own_logits(0)
    own_logits(1)
    for k in range(2):
        for j in range(7):
            cols = pl.ds(j * 256, 256)
            st[j * 256 : (j + 1) * 256, k * 256 : (k + 1) * 256] = s_all[k, :, :, :, cols].reshape(256, 256).T
    s_cp = pltpu.make_async_copy(st, s_out, lsem.at[3])
    s_cp.start()
    ends.append(s_cp.wait)
    for i, d in enumerate((1, 2, 3)):
        z_, x_ = zs_[4 - d], xs[4 - d]
        t3[2 * i].wait_recv()
        r = tb.at[c, pl.ds(0, 2), :, z_]
        sib_t.append(rcopy(r, r, sibling))
        t3[2 * i + 1].wait_recv()
        r = tb.at[c, pl.ds(2, 2), x_]
        sib_t.append(rcopy(r, r, sibling))
    for cp in sib_t:
        cp.wait_recv()

    o = lax.broadcasted_iota(jnp.int32, (256, 256), 0)
    src = lax.broadcasted_iota(jnp.int32, (256, 256), 1)
    o_j, o_r = o // 64, lax.rem(o, 4)
    o_h, o_z = lax.rem(o // 32, 2), lax.rem(o // 16, 2) * 2 + lax.rem(o // 4, 2)
    o_x = lax.rem(o // 8, 2)
    perm = (src == o_h * 128 + o_x * 64 + o_z * 16 + o_j * 4 + o_r).astype(jnp.bfloat16)

    def teacher(k):
        @pl.loop(4 * k, 4 * k + 4)
        def _(g):
            c_, p_, x_ = g // 4, lax.rem(g // 2, 2), lax.rem(g, 2)
            pieces = [tb[c_, 2 * a + p_, 2 * x_ + b].reshape(64, KT) for a in range(2) for b in range(2)]
            out = jnp.dot(perm, jnp.concatenate(pieces, axis=0), preferred_element_type=jnp.float32)
            out = out.astype(jnp.bfloat16)
            for j in range(4):
                tn[pl.ds(pl.multiple_of(g * 64, 64), 64), j * KT : (j + 1) * KT] = out[j * 64 : (j + 1) * 64]

        rows = pl.ds(k * 256, 256)

        @pl.loop(0, 4)
        def _(n):
            cols = pl.ds(pl.multiple_of(n * 256, 256), 256)
            logits = jnp.dot(tn[rows, :], wt[:, cols], preferred_element_type=jnp.float32)
            et[rows, cols] = jnp.exp(CAP * jnp.tanh(logits / CAP))

    teacher(0)
    tw_cp.wait_recv()
    w_nat = [[column(tw2[i, b, 0:1, :]) for b in range(2)] for i in range(2)]
    g_cp = {}
    gcol = pl.ds(pl.multiple_of(p * VT, VT), VT)
    ocol = pl.ds(pl.multiple_of((1 - p) * VT, VT), VT)

    def g_send(k, i):
        region = g_all.at[pl.ds(k * 256 + i * 128, 128), gcol]
        g_cp[k, i] = rcopy(region, region, partner)

    for k in range(2):
        for cp in z_cp[k]:
            cp.wait_recv()
        if k == 0:
            pass
        if k == 1:
            pass
        for i in range(2):
            rows = pl.ds(k * 256 + i * 128, 128)

            @pl.loop(0, 8)
            def _(n):
                cols = pl.ds(pl.multiple_of(n * 128, 128), 128)
                th_ = jnp.tanh((zo[rows, cols] + decode(zr[rows, cols])) / CAP)
                zo[rows, cols] = jnp.exp(CAP * th_)
                slope[rows, cols] = 1.0 - th_ * th_

            ar_s[k, i : i + 1, :] = row_sums(zo[rows, :])
            ar_s[k, 2 + i : 3 + i, :] = row_sums(et[rows, :])
        ar_s[k, 4:8, :] = jnp.zeros((4, 128), jnp.float32)
        if k == 0:
            pass
        rcopy(ar_s.at[k], ar_c.at[k], sibling).wait_recv()
        me_xz = x * 4 + z
        ar_r[k, me_xz] = ar_s[k] + ar_c[k]
        ar_cp = []
        for a, b in plane[1:]:
            mine = ar_r.at[k, me_xz]
            ar_cp.append(rcopy(mine, mine, dev(p, xs[a], c, h, zs_[b])))
        if k == 0:
            teacher(1)
        for cp in ar_cp:
            cp.wait_recv()
        if k == 0:
            pass
        ar_y[k, y] = jnp.sum(ar_r[k], axis=0)
        mine = ar_y.at[k, y]
        ar_cp = [rcopy(mine, mine, ydev[d]) for d in (1, 2, 3)]
        if k == 1:
            g_send(0, 1)
        for cp in ar_cp:
            cp.wait_recv()
        total = jnp.sum(ar_y[k], axis=0)
        if k == 0:
            pass
        if k == 1:
            pass
        for i in range(2):
            rows = pl.ds(k * 256 + i * 128, 128)
            w_col = jnp.concatenate(
                [
                    w_nat[i][b7][b6 * 64 + k * 32 + b43 * 8 :][:8]
                    for b7 in range(2)
                    for b43 in range(4)
                    for b6 in range(2)
                ],
                axis=0,
            )
            s_col = 1.0 / column(total[i : i + 1, :])
            t_col = 1.0 / column(total[2 + i : 3 + i, :])

            @pl.loop(0, 8)
            def _(n):
                cols = pl.ds(pl.multiple_of(n * 128, 128), 128)
                probs = (et[rows, cols] * t_col).astype(jnp.bfloat16).astype(jnp.float32)
                grad = w_col * (zo[rows, cols] * s_col - probs) * slope[rows, cols]
                g_all[rows, pl.ds(pl.multiple_of(p * VT + n * 128, 128), 128)] = grad.astype(jnp.bfloat16)

            if (k, i) != (0, 1):
                g_send(k, i)

    nt = (((1,), (1,)), ((), ()))

    @pl.loop(0, 7)
    def _(n):
        w_rows = pl.ds(pl.multiple_of(n * 256, 256), 256)
        dacc[:, w_rows] = lax.dot_general(g_all[:, gcol], ws[0, w_rows, :], nt, preferred_element_type=jnp.float32)

    rs_sem = counter[0]
    counter[0] += 4
    slot = x * 4 + z
    xcol = pl.ds(pl.multiple_of((1 - c) * CS, 128), CS)

    def rs_send(k, i, a, b):
        x_ = 2 * i + lax.rem(x + a, 2)
        return pltpu.make_async_remote_copy(
            src_ref=rs_s.at[k, x_, zs_[b]], dst_ref=rs_r.at[k, slot],
            send_sem=ssem.at[rs_sem + k], recv_sem=rsem.at[rs_sem + k],
            device_id=dev(p, x_, c, h, zs_[b]), device_id_type=MESH,
        )

    pieces = [(a, b) for b in range(4) for a in range(2)]

    def scatter(k, first, size):
        rows = pl.ds(k * 256 + first, size)

        @pl.loop(0, 7)
        def _(n):
            w_rows = pl.ds(pl.multiple_of(n * 256, 256), 256)
            dacc[rows, w_rows] += lax.dot_general(
                g_all[rows, ocol], ws[1, w_rows, :], nt, preferred_element_type=jnp.float32
            )

        rsib_s[rows, :] = dacc[rows, xcol].astype(jnp.bfloat16)
        rcopy(rsib_s.at[rows], rsib_r.at[rows], sibling).wait_recv()
        both = (dacc[rows, ccol] + rsib_r[rows, :].astype(jnp.float32)).astype(jnp.bfloat16)
        rs_s[k, first // 64 : (first + size) // 64] = both.reshape(size // 64, 4, 16, CS)
        for i in range(first // 128, (first + size) // 128):
            for a, b in pieces[1:]:
                rs_send(k, i, a, b).start()

            @pl.when(x // 2 != i)
            def _():
                rs_send(k, i, 0, 0).start()

            def rs_end(i=i):
                for a, b in pieces[1:]:
                    rs_send(k, i, a, b).wait_send()

                @pl.when(x // 2 != i)
                def _():
                    rs_send(k, i, 0, 0).wait_send()

            ends.append(rs_end)

    def gather_sum(k):
        rwait(rs_r.at[k, pl.ds(0, 15)], rsem.at[rs_sem + k])
        rs_r[k, slot] = rs_s[k, x, z]
        fin_s[k] = jnp.sum(rs_r[k].astype(jnp.float32), axis=0)
        own = fin_s.at[k, pl.ds(pl.multiple_of(c * 8, 8), 8)]
        other = fin_s.at[k, pl.ds(pl.multiple_of((1 - c) * 8, 8), 8)]

        def f_copy(n, src, device):
            return pltpu.make_async_remote_copy(
                src_ref=src, dst_ref=fin.at[c, h], send_sem=ssem.at[fin_sem + n], recv_sem=rsem.at[fin_sem + n],
                device_id=device, device_id_type=MESH,
            )

        @pl.when(h == k)
        def _():
            fin[c, h] = own[...]
            f_copy(0, other, sibling).start()

        @pl.when(h != k)
        def _():
            f_copy(1, own, hdev).start()
            f_copy(2, other, cross).start()

        def f_end():
            @pl.when(h == k)
            def _():
                f_copy(0, other, sibling).wait_send()

            @pl.when(h != k)
            def _():
                f_copy(1, own, hdev).wait_send()
                f_copy(2, other, cross).wait_send()

        ends.append(f_end)

    fin_sem = counter[0]
    counter[0] += 3
    g_cp[0, 0].wait_recv()
    g_cp[0, 1].wait_recv()
    scatter(0, 0, 256)
    g_cp[1, 0].wait_recv()
    scatter(1, 0, 128)
    gather_sum(0)
    g_cp[1, 1].wait_recv()
    scatter(1, 128, 128)
    g_out_cp = pltpu.make_async_copy(g_all, g_out, lsem.at[4])
    g_out_cp.start()
    ends.append(g_out_cp.wait)

    gather_sum(1)
    for n in range(3):
        rwait(fin.at[0, 0], rsem.at[fin_sem + n])
    scaled = jnp.concatenate([fin[0, 0] + fin[0, 1], fin[1, 0] + fin[1, 1]], axis=-1) * gain
    inn[0] = jnp.broadcast_to(jnp.sum(sx * scaled, axis=-1, keepdims=True), (8, 128))
    rcopy(inn.at[0], inn.at[1], partner).wait_recv()
    inner = (inn[0] + inn[1])[:, :1]
    dh_out[...] = stud_r * scaled - sx * (stud_r * stud_r * stud_r) * inner / DS

    finish()


def head(th, tg, sh, sg, tw, wt, ws):
    f32, bf16 = jnp.float32, jnp.bfloat16
    vmem = pl.BlockSpec(memory_space=pltpu.VMEM)
    hbm = pl.BlockSpec(memory_space=pl.ANY)
    scratch = [
        pltpu.VMEM((DT, VT), bf16),
        pltpu.VMEM((2, HS, VT), bf16),
        pltpu.VMEM((16, KT), f32),
        pltpu.VMEM((2, 4, 4, 4, 16, KT), bf16),
        pltpu.VMEM((512, DT), bf16),
        pltpu.VMEM((2, 8, 128), f32),
        pltpu.VMEM((2, 8, CS), f32),
        pltpu.VMEM((16, CS), f32),
        pltpu.VMEM((2, 4, 4, 16, HS), bf16),
        pltpu.VMEM((HS, 512), bf16),
        pltpu.VMEM((512, VT), bf16),
        pltpu.VMEM((512, VT), bf16),
        pltpu.VMEM((512, VT), f32),
        pltpu.VMEM((512, VT), f32),
        pltpu.VMEM((512, VT), f32),
        pltpu.VMEM((512, 2 * VT), bf16),
        pltpu.VMEM((2, 2, 8, 128), f32),
        pltpu.VMEM((2, 8, 128), f32),
        pltpu.VMEM((2, 8, 128), f32),
        pltpu.VMEM((2, 16, 8, 128), f32),
        pltpu.VMEM((2, 4, 8, 128), f32),
        pltpu.VMEM((512, HS), f32),
        pltpu.VMEM((512, CS), bf16),
        pltpu.VMEM((512, CS), bf16),
        pltpu.VMEM((2, 4, 4, 16, CS), bf16),
        pltpu.VMEM((2, 16, 16, CS), bf16),
        pltpu.VMEM((2, 16, CS), f32),
        pltpu.VMEM((2, 2, 8, CS), f32),
        pltpu.VMEM((2, 8, 128), f32),
        pltpu.SemaphoreType.DMA((144,)),
        pltpu.SemaphoreType.DMA((144,)),
        pltpu.SemaphoreType.DMA((5,)),
    ]
    return pl.pallas_call(
        head_kernel,
        out_shape=(
            jax.ShapeDtypeStruct((8, HS), f32),
            jax.ShapeDtypeStruct((HS, 512), bf16),
            jax.ShapeDtypeStruct((512, 2 * VT), bf16),
        ),
        in_specs=[vmem] * 5 + [hbm] * 2,
        out_specs=(vmem, hbm, hbm),
        scratch_shapes=scratch,
        compiler_params=pltpu.CompilerParams(
            collective_id=0, has_side_effects=True, vmem_limit_bytes=58 * 1024 * 1024
        ),
        name="head",
    )(th, tg, sh, sg, tw, wt, ws)


def weight_kernel(s_ref, g_ref, o_ref):
    o_ref[...] = jnp.dot(s_ref[...], g_ref[...], preferred_element_type=jnp.float32).astype(jnp.bfloat16)


def per_device(
    teacher_hidden,
    teacher_gain,
    teacher_weight,
    student_hidden,
    student_gain,
    student_weight,
    token_weight,
):
    d_hidden, s_all, g_all = head(
        teacher_hidden,
        teacher_gain,
        student_hidden,
        student_gain,
        token_weight,
        teacher_weight.reshape(DT, VT),
        student_weight,
    )
    d_weight = pl.pallas_call(
        weight_kernel,
        grid=(HS // 256,),
        in_specs=[pl.BlockSpec((256, 512), lambda i: (i, 0)), pl.BlockSpec((512, 2 * VT), lambda i: (0, 0))],
        out_specs=pl.BlockSpec((256, 2 * VT), lambda i: (i, 0)),
        out_shape=jax.ShapeDtypeStruct((HS, 2 * VT), jnp.bfloat16),
        compiler_params=pltpu.CompilerParams(vmem_limit_bytes=32 * 1024 * 1024),
        name="d_weight",
    )(s_all, g_all)
    return (d_hidden, d_weight)


def solution(mesh):
    return jax.shard_map(
        per_device,
        mesh=mesh,
        in_specs=(
            P(("pair", "vocab", "tok"), None),
            P(),
            P(None, ("vocab", "tok"), "pair", None),
            P(("vocab", "tok"), "pair"),
            P("pair"),
            P("pair", ("vocab", "tok")),
            P("pair"),
        ),
        out_specs=(P(("vocab", "tok"), "pair"), P("pair", ("vocab", "tok"))),
        check_vma=False,
    )
```

```python
import jax
import jax.numpy as jnp
from jax import lax
from jax.experimental import pallas as pl
from jax.experimental.pallas import tpu as pltpu
from jax.sharding import PartitionSpec as P

DT = 4608
DS = 3584
HS = DS // 2
CS = HS // 2
VT = 1024
EPS = 1e-06
CAP = 30.0
KT = DT // 4
MESH = pl.DeviceIdType.MESH

SLOPE = 3.0
KNEE = 64.0
LOGK = 7.2
BIAS = 125.0
LOG2E = 1.4426950408889634


def encode(b):
    a = jnp.abs(b)
    far = SLOPE * KNEE + LOGK * LOG2E * jnp.log(jnp.maximum(a, KNEE) / KNEE)
    w = jnp.where(a <= KNEE, SLOPE * a, jnp.minimum(far, 251.5)) - BIAS
    y = jnp.exp2(w)
    return jnp.where(b < 0, -y, y).astype(jnp.bfloat16)


def decode(code):
    y = code.astype(jnp.float32)
    w = jnp.log(jnp.abs(y)) * LOG2E + BIAS
    a = jnp.where(
        w <= SLOPE * KNEE,
        jnp.maximum(w, 0.0) * (1.0 / SLOPE),
        KNEE * jnp.exp2((w - SLOPE * KNEE) * (1.0 / LOGK)),
    )
    return jnp.where(y < 0, -a, a)


def row_sums(e):
    part = e[:, :128]
    for n in range(1, e.shape[1] // 128):
        part = part + e[:, n * 128 : (n + 1) * 128]
    return jnp.sum(part.T, axis=0, keepdims=True)


def column(row):
    return jnp.broadcast_to(row, (128, 128)).T


def head_kernel(
    th, tg, sh, sg, tw, wt_hbm, ws_hbm,
    dh_out, st_out, g_out, dw_own,
    wt, ws, tsc, tb, tn, sq, nf, raw, s_all, st, zs, zr, zo, slope, et, g_all, tw2,
    ar_s, ar_c, ar_r, ar_y, dacc, rsib_s, rsib_r, rs_s, rs_r, fin_s, fin, inn,
    ssem, rsem, lsem,
):
    p = lax.axis_index("pair")
    v = lax.axis_index("vocab")
    t = lax.axis_index("tok")
    x, c, h, z = v // 2, lax.rem(v, 2), t // 4, lax.rem(t, 4)
    y = 2 * h + p

    def dev(p_, x_, c_, h_, z_):
        return (p_, 2 * x_ + c_, 4 * h_ + z_)

    partner = dev(1 - p, x, c, h, z)
    sibling = dev(p, x, 1 - c, h, z)
    xs = [x] + [lax.rem(x + d, 4) for d in (1, 2, 3)]
    zs_ = [z] + [lax.rem(z + d, 4) for d in (1, 2, 3)]
    xdev = [dev(p, xs[d], c, h, z) for d in range(4)]
    zdev = [dev(p, x, c, h, zs_[d]) for d in range(4)]
    ys = [y] + [lax.rem(y + d, 4) for d in (1, 2, 3)]
    ydev = [dev(lax.rem(ys[d], 2), x, c, ys[d] // 2, z) for d in range(4)]
    hdev = ydev[2]
    cross = dev(p, x, 1 - c, 1 - h, z)
    group = [
        dev(1 - p if a else p, x, 1 - c if b else c, 1 - h if e else h, z)
        for a in range(2)
        for b in range(2)
        for e in range(2)
    ]
    plane = [(a, b) for b in range(4) for a in range(4)]

    counter = [0]
    sends = []
    ends = []

    class Copy:
        def __init__(self, i, src, dst, device):
            self.cp = pltpu.make_async_remote_copy(
                src_ref=src, dst_ref=dst, send_sem=ssem.at[i], recv_sem=rsem.at[i],
                device_id=device, device_id_type=MESH,
            )
            self.cp.start()
            self.here = False

        def wait_recv(self):
            if not self.here:
                self.cp.wait_recv()
            self.here = True

    def rcopy(src, dst, device):
        i = counter[0]
        counter[0] += 1
        sends.append(Copy(i, src, dst, device))
        return sends[-1]

    def finish():
        for cp in sends:
            cp.wait_recv()
            cp.cp.wait_send()
        for end in ends:
            end()

    def rwait(region, sem):
        pltpu.make_async_remote_copy(
            src_ref=region, dst_ref=region, send_sem=sem, recv_sem=sem,
            device_id=partner, device_id_type=MESH,
        ).wait_recv()

    w_cp = [
        pltpu.make_async_copy(ws_hbm.at[:, pl.ds(pl.multiple_of((1 - p) * VT, VT), VT)], ws.at[1], lsem.at[0]),
        pltpu.make_async_copy(ws_hbm.at[:, pl.ds(pl.multiple_of(p * VT, VT), VT)], ws.at[0], lsem.at[1]),
        pltpu.make_async_copy(wt_hbm, wt, lsem.at[2]),
    ]
    for cp in w_cp:
        cp.start()
    w_here = []

    def w_wait():
        if not w_here:
            for cp in w_cp:
                cp.wait()
        w_here.append(True)

    ends.append(w_wait)

    bar = pltpu.get_barrier_semaphore()
    for d in group[1:]:
        pl.semaphore_signal(bar, inc=1, device_id=d, device_id_type=MESH)
    for a, b in plane[1:]:
        pl.semaphore_signal(bar, inc=1, device_id=dev(p, xs[a], c, h, zs_[b]), device_id_type=MESH)

    sx = sh[...].astype(jnp.float32)
    sq[p, c, h] = jnp.broadcast_to(jnp.sum(sx * sx, axis=-1, keepdims=True), (8, 128))
    nf[0] = sx[:, :CS]
    nf[1] = sx[:, CS:]
    mine = raw.at[h, pl.ds(pl.multiple_of(c * 8, 8), 8)]
    mine[...] = nf[c]
    tx = th[...].astype(jnp.float32)
    tnorm = tx * lax.rsqrt(jnp.mean(tx * tx, axis=-1, keepdims=True) + EPS) * tg[...].reshape(1, DT)
    for j in range(4):
        tsc[4 * j : 4 * j + 4, :] = tnorm[:, j * KT : (j + 1) * KT]
    tb[c, y, x, z] = tsc[...].astype(jnp.bfloat16)
    for b in range(2):
        tw2[p, b] = jnp.broadcast_to(tw[pl.ds(128 * b, 128)].reshape(1, 128), (8, 128))

    pl.semaphore_wait(bar, 22)

    first = [
        rcopy(nf.at[1 - c], mine, sibling),
        rcopy(nf.at[c], mine, hdev),
        rcopy(nf.at[1 - c], mine, cross),
    ]
    first += [rcopy(sq.at[p, c, h], sq.at[p, c, h], d) for d in group[1:]]
    own_t = tb.at[c, y, x, z]
    t1 = [rcopy(own_t, own_t, ydev[d]) for d in (1, 2, 3)]
    tw_cp = rcopy(tw2.at[p], tw2.at[p], partner)
    gain = sg[...].reshape(1, HS)
    gain_c = jnp.where(c == 0, gain[:, :CS], gain[:, CS:])
    ccol = pl.ds(pl.multiple_of(c * CS, 128), CS)
    for cp in first:
        cp.wait_recv()
    for h_ in range(2):
        tile = []
        for c_ in range(2):
            scale = lax.rsqrt((sq[0, c_, h_] + sq[1, c_, h_])[:, :1] / DS + EPS)
            tile.append(raw[h_, 8 * c_ : 8 * c_ + 8] * scale * gain_c)
        s_all[h_, x, z, :, ccol] = jnp.concatenate(tile, axis=0).astype(jnp.bfloat16)
    stud_r = lax.rsqrt((sq[0, c, h] + sq[1, c, h])[:, :1] / DS + EPS)
    s2 = []
    for d in (1, 2, 3):
        a, b = s_all.at[0, x, z, :, ccol], s_all.at[1, x, z, :, ccol]
        s2.append(rcopy(a, a, xdev[d]))
        s2.append(rcopy(b, b, zdev[d]))
    for cp in t1:
        cp.wait_recv()
    t2 = []
    for d in (1, 2, 3):
        a, b = tb.at[c, pl.ds(0, 2), x, z], tb.at[c, pl.ds(2, 2), x, z]
        t2.append(rcopy(a, a, xdev[d]))
        t2.append(rcopy(b, b, zdev[d]))
    for cp in s2:
        cp.wait_recv()
    s3 = []
    for d in (1, 2, 3):
        a, b = s_all.at[0, :, z, :, ccol], s_all.at[1, x, :, :, ccol]
        s3.append(rcopy(a, a, zdev[d]))
        s3.append(rcopy(b, b, xdev[d]))
    for cp in t2:
        cp.wait_recv()
    t3 = ([], [])
    for i in range(2):
        for d in (1, 2, 3):
            a, b = tb.at[c, i, :, z], tb.at[c, 2 + i, x]
            t3[i].append(rcopy(a, a, zdev[d]))
            t3[i].append(rcopy(b, b, xdev[d]))
    sib_t = []
    for r in (tb.at[c, pl.ds(0, 2), :, z], tb.at[c, pl.ds(2, 2), x]):
        sib_t.append(rcopy(r, r, sibling))
    sib_s = ([], [])
    for i in range(4):
        if i:
            s3[2 * i - 2].wait_recv()
        r = s_all.at[0, :, zs_[(4 - i) % 4], :, ccol]
        sib_s[0].append(rcopy(r, r, sibling))
    for i in range(4):
        if i:
            s3[2 * i - 1].wait_recv()
        r = s_all.at[1, xs[(4 - i) % 4], :, :, ccol]
        sib_s[1].append(rcopy(r, r, sibling))
    w_wait()

    z_cp = ([], [])
    for k in range(2):
        for cp in sib_s[k]:
            cp.wait_recv()
        rows = pl.ds(k * 256, 256)
        lhs = s_all[k].reshape(256, HS)
        for n in range(4):
            cols = pl.ds(n * 256, 256)
            zs[rows, cols] = encode(jnp.dot(lhs, ws[1, :, cols], preferred_element_type=jnp.float32))
            z_cp[k].append(rcopy(zs.at[rows, cols], zr.at[rows, cols], partner))
    def forward(i):
        for d in (1, 2, 3):
            t3[i][2 * d - 2].wait_recv()
            r = tb.at[c, i, :, zs_[4 - d]]
            sib_t.append(rcopy(r, r, sibling))
            t3[i][2 * d - 1].wait_recv()
            r = tb.at[c, 2 + i, xs[4 - d]]
            sib_t.append(rcopy(r, r, sibling))

    forward(0)


    def own_logits(k):
        rows = pl.ds(k * 256, 256)

        @pl.loop(0, 4)
        def _(n):
            cols = pl.ds(pl.multiple_of(n * 256, 256), 256)
            zo[rows, cols] = jnp.dot(s_all[k].reshape(256, HS), ws[0, :, cols], preferred_element_type=jnp.float32)

    own_logits(0)
    for k in range(2):
        for j in range(7):
            cols = pl.ds(j * 256, 256)
            st[j * 256 : (j + 1) * 256, k * 256 : (k + 1) * 256] = s_all[k, :, :, :, cols].reshape(256, 256).T
    st_cp = pltpu.make_async_copy(st, st_out, lsem.at[3])
    st_cp.start()
    ends.append(st_cp.wait)
    forward(1)
    own_logits(1)
    for cp in sib_t:
        cp.wait_recv()

    o = lax.broadcasted_iota(jnp.int32, (256, 256), 0)
    src = lax.broadcasted_iota(jnp.int32, (256, 256), 1)
    o_j, o_r = o // 64, lax.rem(o, 4)
    o_h, o_z = lax.rem(o // 32, 2), lax.rem(o // 16, 2) * 2 + lax.rem(o // 4, 2)
    o_x = lax.rem(o // 8, 2)
    perm = (src == o_h * 128 + o_x * 64 + o_z * 16 + o_j * 4 + o_r).astype(jnp.bfloat16)

    def permute(k):
        @pl.loop(4 * k, 4 * k + 4)
        def _(g):
            c_, p_, x_ = g // 4, lax.rem(g // 2, 2), lax.rem(g, 2)
            pieces = [tb[c_, 2 * a + p_, 2 * x_ + b].reshape(64, KT) for a in range(2) for b in range(2)]
            out = jnp.dot(perm, jnp.concatenate(pieces, axis=0), preferred_element_type=jnp.float32)
            out = out.astype(jnp.bfloat16)
            for j in range(4):
                tn[pl.ds(pl.multiple_of(g * 64, 64), 64), j * KT : (j + 1) * KT] = out[j * 64 : (j + 1) * 64]

    def teacher(k):
        rows = pl.ds(k * 256, 256)

        @pl.loop(0, 4)
        def _(n):
            cols = pl.ds(pl.multiple_of(n * 256, 256), 256)
            logits = jnp.dot(tn[rows, :], wt[:, cols], preferred_element_type=jnp.float32)
            et[rows, cols] = jnp.exp(CAP * jnp.tanh(logits / CAP))

    permute(0)
    teacher(0)
    tw_cp.wait_recv()
    w_nat = [[column(tw2[i, b, 0:1, :]) for b in range(2)] for i in range(2)]
    g_cp = {}
    gcol = pl.ds(pl.multiple_of(p * VT, VT), VT)
    ocol = pl.ds(pl.multiple_of((1 - p) * VT, VT), VT)

    def g_send(k, i):
        region = g_all.at[pl.ds(k * 256 + i * 128, 128), gcol]
        g_cp[k, i] = rcopy(region, region, partner)

    me_xz = x * 4 + z

    def exps(k):
        for cp in z_cp[k]:
            cp.wait_recv()
        for i in range(2):
            rows = pl.ds(k * 256 + i * 128, 128)

            @pl.loop(0, 8)
            def _(n):
                cols = pl.ds(pl.multiple_of(n * 128, 128), 128)
                th_ = jnp.tanh((zo[rows, cols] + decode(zr[rows, cols])) / CAP)
                zo[rows, cols] = jnp.exp(CAP * th_)
                slope[rows, cols] = 1.0 - th_ * th_

            ar_s[k, i : i + 1, :] = row_sums(zo[rows, :])
            ar_s[k, 2 + i : 3 + i, :] = row_sums(et[rows, :])
        ar_s[k, 4:8, :] = jnp.zeros((4, 128), jnp.float32)
        return rcopy(ar_s.at[k], ar_c.at[k], sibling)

    def to_plane(k, cp):
        cp.wait_recv()
        ar_r[k, me_xz] = ar_s[k] + ar_c[k]
        mine = ar_r.at[k, me_xz]
        return [rcopy(mine, mine, dev(p, xs[a], c, h, zs_[b])) for a, b in plane[1:]]

    def to_column(k, cps):
        for cp in cps:
            cp.wait_recv()
        ar_y[k, y] = jnp.sum(ar_r[k], axis=0)
        mine = ar_y.at[k, y]
        return [rcopy(mine, mine, ydev[d]) for d in (1, 2, 3)]

    def total(k, cps):
        for cp in cps:
            cp.wait_recv()
        return jnp.sum(ar_y[k], axis=0)

    def grads(k, i, totals):
        rows = pl.ds(k * 256 + i * 128, 128)
        w_col = jnp.concatenate(
            [
                w_nat[i][b7][b6 * 64 + k * 32 + b43 * 8 :][:8]
                for b7 in range(2)
                for b43 in range(4)
                for b6 in range(2)
            ],
            axis=0,
        )
        s_col = 1.0 / column(totals[i : i + 1, :])
        t_col = 1.0 / column(totals[2 + i : 3 + i, :])

        @pl.loop(0, 8)
        def _(n):
            cols = pl.ds(pl.multiple_of(n * 128, 128), 128)
            probs = (et[rows, cols] * t_col).astype(jnp.bfloat16).astype(jnp.float32)
            grad = w_col * (zo[rows, cols] * s_col - probs) * slope[rows, cols]
            g_all[rows, pl.ds(pl.multiple_of(p * VT + n * 128, 128), 128)] = grad.astype(jnp.bfloat16)

    sib0 = exps(0)
    plane0 = to_plane(0, sib0)
    permute(1)
    column0 = to_column(0, plane0)
    teacher(1)
    sib1 = exps(1)
    totals = total(0, column0)
    grads(0, 0, totals)
    g_send(0, 0)
    plane1 = to_plane(1, sib1)
    grads(0, 1, totals)
    column1 = to_column(1, plane1)
    g_send(0, 1)
    totals = total(1, column1)
    for i in range(2):
        grads(1, i, totals)
        g_send(1, i)

    nt = (((1,), (1,)), ((), ()))

    def own_grad(k):
        rows = pl.ds(k * 256, 256)

        @pl.loop(0, 7)
        def _(n):
            w_rows = pl.ds(pl.multiple_of(n * 256, 256), 256)
            dacc[rows, w_rows] = lax.dot_general(
                g_all[rows, gcol], ws[0, w_rows, :], nt, preferred_element_type=jnp.float32
            )

    own_grad(0)
    own_grad(1)
    rs_sem = counter[0]
    counter[0] += 4
    slot = x * 4 + z
    xcol = pl.ds(pl.multiple_of((1 - c) * CS, 128), CS)

    def rs_send(k, i, a, b):
        x_ = 2 * i + lax.rem(x + a, 2)
        return pltpu.make_async_remote_copy(
            src_ref=rs_s.at[k, x_, zs_[b]], dst_ref=rs_r.at[k, slot],
            send_sem=ssem.at[rs_sem + k], recv_sem=rsem.at[rs_sem + k],
            device_id=dev(p, x_, c, h, zs_[b]), device_id_type=MESH,
        )

    pieces = [(a, b) for b in range(4) for a in range(2)]

    def scatter(k, first, size):
        rows = pl.ds(k * 256 + first, size)

        @pl.loop(0, 7)
        def _(n):
            w_rows = pl.ds(pl.multiple_of(n * 256, 256), 256)
            dacc[rows, w_rows] += lax.dot_general(
                g_all[rows, ocol], ws[1, w_rows, :], nt, preferred_element_type=jnp.float32
            )

        rsib_s[rows, :] = dacc[rows, xcol].astype(jnp.bfloat16)
        rcopy(rsib_s.at[rows], rsib_r.at[rows], sibling).wait_recv()
        both = (dacc[rows, ccol] + rsib_r[rows, :].astype(jnp.float32)).astype(jnp.bfloat16)
        rs_s[k, first // 64 : (first + size) // 64] = both.reshape(size // 64, 4, 16, CS)
        for i in range(first // 128, (first + size) // 128):
            for a, b in pieces[1:]:
                rs_send(k, i, a, b).start()

            @pl.when(x // 2 != i)
            def _():
                rs_send(k, i, 0, 0).start()

            def rs_end(i=i):
                for a, b in pieces[1:]:
                    rs_send(k, i, a, b).wait_send()

                @pl.when(x // 2 != i)
                def _():
                    rs_send(k, i, 0, 0).wait_send()

            ends.append(rs_end)

    def gather_sum(k):
        rwait(rs_r.at[k, pl.ds(0, 15)], rsem.at[rs_sem + k])
        rs_r[k, slot] = rs_s[k, x, z]
        fin_s[k] = jnp.sum(rs_r[k].astype(jnp.float32), axis=0)
        own = fin_s.at[k, pl.ds(pl.multiple_of(c * 8, 8), 8)]
        other = fin_s.at[k, pl.ds(pl.multiple_of((1 - c) * 8, 8), 8)]

        def f_copy(n, src, device):
            return pltpu.make_async_remote_copy(
                src_ref=src, dst_ref=fin.at[c, h], send_sem=ssem.at[fin_sem + n], recv_sem=rsem.at[fin_sem + n],
                device_id=device, device_id_type=MESH,
            )

        @pl.when(h == k)
        def _():
            fin[c, h] = own[...]
            f_copy(0, other, sibling).start()

        @pl.when(h != k)
        def _():
            f_copy(1, own, hdev).start()
            f_copy(2, other, cross).start()

        def f_end():
            @pl.when(h == k)
            def _():
                f_copy(0, other, sibling).wait_send()

            @pl.when(h != k)
            def _():
                f_copy(1, own, hdev).wait_send()
                f_copy(2, other, cross).wait_send()

        ends.append(f_end)

    fin_sem = counter[0]
    counter[0] += 3
    g_cp[0, 0].wait_recv()
    g_cp[0, 1].wait_recv()
    scatter(0, 0, 256)

    @pl.loop(0, 7)
    def _(n):
        rows = pl.ds(pl.multiple_of(n * 256, 256), 256)
        wt[rows, :] = jnp.dot(st[rows, :], g_all[:, gcol], preferred_element_type=jnp.float32).astype(jnp.bfloat16)

    dw_cp = pltpu.make_async_copy(wt.at[pl.ds(0, HS)], dw_own, lsem.at[5])
    dw_cp.start()
    ends.append(dw_cp.wait)
    g_cp[1, 0].wait_recv()
    scatter(1, 0, 128)
    g_cp[1, 1].wait_recv()
    scatter(1, 128, 128)
    gather_sum(0)
    g_out_cp = pltpu.make_async_copy(g_all.at[:, ocol], g_out, lsem.at[4])
    g_out_cp.start()
    ends.append(g_out_cp.wait)
    gather_sum(1)
    for n in range(3):
        rwait(fin.at[0, 0], rsem.at[fin_sem + n])
    scaled = jnp.concatenate([fin[0, 0] + fin[0, 1], fin[1, 0] + fin[1, 1]], axis=-1) * gain
    inn[0] = jnp.broadcast_to(jnp.sum(sx * scaled, axis=-1, keepdims=True), (8, 128))
    rcopy(inn.at[0], inn.at[1], partner).wait_recv()
    inner = (inn[0] + inn[1])[:, :1]
    dh_out[...] = stud_r * scaled - sx * (stud_r * stud_r * stud_r) * inner / DS

    finish()


def head(th, tg, sh, sg, tw, wt, ws):
    f32, bf16 = jnp.float32, jnp.bfloat16
    vmem = pl.BlockSpec(memory_space=pltpu.VMEM)
    hbm = pl.BlockSpec(memory_space=pl.ANY)
    scratch = [
        pltpu.VMEM((DT, VT), bf16),
        pltpu.VMEM((2, HS, VT), bf16),
        pltpu.VMEM((16, KT), f32),
        pltpu.VMEM((2, 4, 4, 4, 16, KT), bf16),
        pltpu.VMEM((512, DT), bf16),
        pltpu.VMEM((2, 2, 2, 8, 128), f32),
        pltpu.VMEM((2, 8, CS), f32),
        pltpu.VMEM((2, 16, CS), f32),
        pltpu.VMEM((2, 4, 4, 16, HS), bf16),
        pltpu.VMEM((HS, 512), bf16),
        pltpu.VMEM((512, VT), bf16),
        pltpu.VMEM((512, VT), bf16),
        pltpu.VMEM((512, VT), f32),
        pltpu.VMEM((512, VT), f32),
        pltpu.VMEM((512, VT), f32),
        pltpu.VMEM((512, 2 * VT), bf16),
        pltpu.VMEM((2, 2, 8, 128), f32),
        pltpu.VMEM((2, 8, 128), f32),
        pltpu.VMEM((2, 8, 128), f32),
        pltpu.VMEM((2, 16, 8, 128), f32),
        pltpu.VMEM((2, 4, 8, 128), f32),
        pltpu.VMEM((512, HS), f32),
        pltpu.VMEM((512, CS), bf16),
        pltpu.VMEM((512, CS), bf16),
        pltpu.VMEM((2, 4, 4, 16, CS), bf16),
        pltpu.VMEM((2, 16, 16, CS), bf16),
        pltpu.VMEM((2, 16, CS), f32),
        pltpu.VMEM((2, 2, 8, CS), f32),
        pltpu.VMEM((2, 8, 128), f32),
        pltpu.SemaphoreType.DMA((144,)),
        pltpu.SemaphoreType.DMA((144,)),
        pltpu.SemaphoreType.DMA((6,)),
    ]
    return pl.pallas_call(
        head_kernel,
        out_shape=(
            jax.ShapeDtypeStruct((8, HS), f32),
            jax.ShapeDtypeStruct((HS, 512), bf16),
            jax.ShapeDtypeStruct((512, VT), bf16),
            jax.ShapeDtypeStruct((HS, VT), bf16),
        ),
        in_specs=[vmem] * 5 + [hbm] * 2,
        out_specs=(vmem, hbm, hbm, hbm),
        scratch_shapes=scratch,
        compiler_params=pltpu.CompilerParams(
            collective_id=0, has_side_effects=True, vmem_limit_bytes=58 * 1024 * 1024
        ),
        name="head",
    )(th, tg, sh, sg, tw, wt, ws)


def weight_kernel(dh_ref, own_hbm, st_hbm, g_hbm, dh_out, dw_out, st, g, own, other, in_sem, out_sem):
    p = lax.axis_index("pair")
    blocks = [pl.ds(256 * i, 256) for i in range(7)]
    own_cols = pl.ds(pl.multiple_of(p * VT, VT), VT)
    other_cols = pl.ds(pl.multiple_of((1 - p) * VT, VT), VT)
    g_in = pltpu.make_async_copy(g_hbm, g, in_sem.at[0])
    st_in = [pltpu.make_async_copy(st_hbm.at[b], st.at[b], in_sem.at[1 + i]) for i, b in enumerate(blocks)]
    own_in = [pltpu.make_async_copy(own_hbm.at[b], own.at[b], in_sem.at[8 + i]) for i, b in enumerate(blocks)]
    for cp in [g_in, *st_in, *own_in]:
        cp.start()
    dh_out[...] = dh_ref[...]
    g_in.wait()
    done = []
    for i, b in enumerate(blocks):
        st_in[i].wait()
        other[b, :] = jnp.dot(st[b, :], g[...], preferred_element_type=jnp.float32).astype(jnp.bfloat16)
        done.append(pltpu.make_async_copy(other.at[b], dw_out.at[b, other_cols], out_sem.at[i]))
        done[-1].start()
        own_in[i].wait()
        done.append(pltpu.make_async_copy(own.at[b], dw_out.at[b, own_cols], out_sem.at[7 + i]))
        done[-1].start()
    for cp in done:
        cp.wait()


def finish_weight(d_hidden, own, st, g):
    vmem = pl.BlockSpec(memory_space=pltpu.VMEM)
    hbm = pl.BlockSpec(memory_space=pl.ANY)
    return pl.pallas_call(
        weight_kernel,
        out_shape=(
            jax.ShapeDtypeStruct((8, HS), jnp.float32),
            jax.ShapeDtypeStruct((HS, 2 * VT), jnp.bfloat16),
        ),
        in_specs=[vmem, hbm, hbm, hbm],
        out_specs=(vmem, hbm),
        scratch_shapes=[
            pltpu.VMEM((HS, 512), jnp.bfloat16),
            pltpu.VMEM((512, VT), jnp.bfloat16),
            pltpu.VMEM((HS, VT), jnp.bfloat16),
            pltpu.VMEM((HS, VT), jnp.bfloat16),
            pltpu.SemaphoreType.DMA((15,)),
            pltpu.SemaphoreType.DMA((14,)),
        ],
        compiler_params=pltpu.CompilerParams(vmem_limit_bytes=58 * 1024 * 1024),
        name="weight",
    )(d_hidden, own, st, g)


def per_device(
    teacher_hidden,
    teacher_gain,
    teacher_weight,
    student_hidden,
    student_gain,
    student_weight,
    token_weight,
):
    d_hidden, st, g, own = head(
        teacher_hidden,
        teacher_gain,
        student_hidden,
        student_gain,
        token_weight,
        teacher_weight.reshape(DT, VT),
        student_weight,
    )
    return finish_weight(d_hidden, own, st, g)


def solution(mesh):
    return jax.shard_map(
        per_device,
        mesh=mesh,
        in_specs=(
            P(("pair", "vocab", "tok"), None),
            P(),
            P(None, ("vocab", "tok"), "pair", None),
            P(("vocab", "tok"), "pair"),
            P("pair"),
            P("pair", ("vocab", "tok")),
            P("pair"),
        ),
        out_specs=(P(("vocab", "tok"), "pair"), P("pair", ("vocab", "tok"))),
        check_vma=False,
    )
```

```python
import jax
import jax.numpy as jnp
from jax import lax
from jax.experimental import pallas as pl
from jax.experimental.pallas import tpu as pltpu
from jax.sharding import PartitionSpec as P

DT = 4608
DS = 3584
HS = DS // 2
CS = HS // 2
VT = 1024
EPS = 1e-06
CAP = 30.0
KT = DT // 4
MESH = pl.DeviceIdType.MESH

SLOPE = 3.0
KNEE = 64.0
LOGK = 7.2
BIAS = 125.0
LOG2E = 1.4426950408889634


def encode(b):
    a = jnp.abs(b)
    far = SLOPE * KNEE + LOGK * LOG2E * jnp.log(jnp.maximum(a, KNEE) / KNEE)
    w = jnp.where(a <= KNEE, SLOPE * a, jnp.minimum(far, 251.5)) - BIAS
    y = jnp.exp2(w)
    return jnp.where(b < 0, -y, y).astype(jnp.bfloat16)


def decode(code):
    y = code.astype(jnp.float32)
    w = jnp.log(jnp.abs(y)) * LOG2E + BIAS
    a = jnp.where(
        w <= SLOPE * KNEE,
        jnp.maximum(w, 0.0) * (1.0 / SLOPE),
        KNEE * jnp.exp2((w - SLOPE * KNEE) * (1.0 / LOGK)),
    )
    return jnp.where(y < 0, -a, a)


def row_sums(e):
    part = e[:, :128]
    for n in range(1, e.shape[1] // 128):
        part = part + e[:, n * 128 : (n + 1) * 128]
    return jnp.sum(part.T, axis=0, keepdims=True)


def column(row):
    return jnp.broadcast_to(row, (128, 128)).T


def head_kernel(
    th, tg, sh, sg, tw, wt_hbm, ws_hbm,
    dh_out, st_out, g_out, dw_own,
    wt, ws, tsc, tb, tn, sq, nf, raw, s_all, st, zs, zr, zo, slope, et, g_all, tw2,
    ar_s, ar_c, ar_r, ar_y, dacc, rsib_s, rsib_r, rs_s, rs_r, fin_s, fin, zp, aq_s, aq_c, aq_r, aq_y, q_sum, q_col,
    ssem, rsem, lsem,
):
    p = lax.axis_index("pair")
    v = lax.axis_index("vocab")
    t = lax.axis_index("tok")
    x, c, h, z = v // 2, lax.rem(v, 2), t // 4, lax.rem(t, 4)
    y = 2 * h + p

    def dev(p_, x_, c_, h_, z_):
        return (p_, 2 * x_ + c_, 4 * h_ + z_)

    partner = dev(1 - p, x, c, h, z)
    sibling = dev(p, x, 1 - c, h, z)
    xs = [x] + [lax.rem(x + d, 4) for d in (1, 2, 3)]
    zs_ = [z] + [lax.rem(z + d, 4) for d in (1, 2, 3)]
    xdev = [dev(p, xs[d], c, h, z) for d in range(4)]
    zdev = [dev(p, x, c, h, zs_[d]) for d in range(4)]
    ys = [y] + [lax.rem(y + d, 4) for d in (1, 2, 3)]
    ydev = [dev(lax.rem(ys[d], 2), x, c, ys[d] // 2, z) for d in range(4)]
    hdev = ydev[2]
    cross = dev(p, x, 1 - c, 1 - h, z)
    group = [
        dev(1 - p if a else p, x, 1 - c if b else c, 1 - h if e else h, z)
        for a in range(2)
        for b in range(2)
        for e in range(2)
    ]
    plane = [(a, b) for b in range(4) for a in range(4)]

    counter = [0]
    sends = []
    ends = []

    class Copy:
        def __init__(self, i, src, dst, device):
            self.cp = pltpu.make_async_remote_copy(
                src_ref=src, dst_ref=dst, send_sem=ssem.at[i], recv_sem=rsem.at[i],
                device_id=device, device_id_type=MESH,
            )
            self.here = False

        def wait_recv(self):
            if not self.here:
                self.cp.wait_recv()
            self.here = True

    def rcopy(src, dst, device, start=True):
        i = counter[0]
        counter[0] += 1
        sends.append(Copy(i, src, dst, device))
        if start:
            sends[-1].cp.start()
        return sends[-1]

    def finish():
        for cp in sends:
            cp.wait_recv()
            cp.cp.wait_send()
        for end in ends:
            end()

    def rwait(region, sem):
        pltpu.make_async_remote_copy(
            src_ref=region, dst_ref=region, send_sem=sem, recv_sem=sem,
            device_id=partner, device_id_type=MESH,
        ).wait_recv()

    w_cp = [
        pltpu.make_async_copy(ws_hbm.at[:, pl.ds(pl.multiple_of((1 - p) * VT, VT), VT)], ws.at[1], lsem.at[0]),
        pltpu.make_async_copy(ws_hbm.at[:, pl.ds(pl.multiple_of(p * VT, VT), VT)], ws.at[0], lsem.at[1]),
        pltpu.make_async_copy(wt_hbm, wt, lsem.at[2]),
    ]
    for cp in w_cp:
        cp.start()
    w_here = []

    def w_wait():
        if not w_here:
            for cp in w_cp:
                cp.wait()
        w_here.append(True)

    ends.append(w_wait)

    bar = pltpu.get_barrier_semaphore()
    for d in group[1:]:
        pl.semaphore_signal(bar, inc=1, device_id=d, device_id_type=MESH)
    for a, b in plane[1:]:
        pl.semaphore_signal(bar, inc=1, device_id=dev(p, xs[a], c, h, zs_[b]), device_id_type=MESH)

    sx = sh[...].astype(jnp.float32)
    sq[p, c, h] = jnp.broadcast_to(jnp.sum(sx * sx, axis=-1, keepdims=True), (8, 128))
    nf[0] = sx[:, :CS]
    nf[1] = sx[:, CS:]
    mine = raw.at[h, pl.ds(pl.multiple_of(c * 8, 8), 8)]
    mine[...] = nf[c]
    tx = th[...].astype(jnp.float32)
    tnorm = tx * lax.rsqrt(jnp.mean(tx * tx, axis=-1, keepdims=True) + EPS) * tg[...].reshape(1, DT)
    for j in range(4):
        tsc[4 * j : 4 * j + 4, :] = tnorm[:, j * KT : (j + 1) * KT]
    tb[c, y, x, z] = tsc[...].astype(jnp.bfloat16)
    for b in range(2):
        tw2[p, b] = jnp.broadcast_to(tw[pl.ds(128 * b, 128)].reshape(1, 128), (8, 128))

    pl.semaphore_wait(bar, 22)

    first = [
        rcopy(nf.at[1 - c], mine, sibling),
        rcopy(nf.at[c], mine, hdev),
        rcopy(nf.at[1 - c], mine, cross),
    ]
    first += [rcopy(sq.at[p, c, h], sq.at[p, c, h], d) for d in group[1:]]
    own_t = tb.at[c, y, x, z]
    t1 = [rcopy(own_t, own_t, ydev[d]) for d in (1, 2, 3)]
    tw_cp = rcopy(tw2.at[p], tw2.at[p], partner)
    gain = sg[...].reshape(1, HS)
    gain_c = jnp.where(c == 0, gain[:, :CS], gain[:, CS:])
    ccol = pl.ds(pl.multiple_of(c * CS, 128), CS)
    for cp in first:
        cp.wait_recv()
    for h_ in range(2):
        tile = []
        for c_ in range(2):
            scale = lax.rsqrt((sq[0, c_, h_] + sq[1, c_, h_])[:, :1] / DS + EPS)
            tile.append(raw[h_, 8 * c_ : 8 * c_ + 8] * scale * gain_c)
        s_all[h_, x, z, :, ccol] = jnp.concatenate(tile, axis=0).astype(jnp.bfloat16)
    stud_r = lax.rsqrt((sq[0, c, h] + sq[1, c, h])[:, :1] / DS + EPS)
    s2 = []
    for d in (1, 2, 3):
        a, b = s_all.at[0, x, z, :, ccol], s_all.at[1, x, z, :, ccol]
        s2.append(rcopy(a, a, xdev[d]))
        s2.append(rcopy(b, b, zdev[d]))
    for cp in t1:
        cp.wait_recv()
    t2 = []
    for d in (1, 2, 3):
        a, b = tb.at[c, pl.ds(0, 2), x, z], tb.at[c, pl.ds(2, 2), x, z]
        t2.append(rcopy(a, a, xdev[d]))
        t2.append(rcopy(b, b, zdev[d]))
    for cp in s2:
        cp.wait_recv()
    s3 = []
    for d in (1, 2, 3):
        a, b = s_all.at[0, :, z, :, ccol], s_all.at[1, x, :, :, ccol]
        s3.append(rcopy(a, a, zdev[d]))
        s3.append(rcopy(b, b, xdev[d]))
    for cp in t2:
        cp.wait_recv()
    sib_t = []
    for r in (tb.at[c, pl.ds(0, 2), :, z], tb.at[c, pl.ds(2, 2), x]):
        sib_t.append(rcopy(r, r, sibling))
    t3, t_on = [], []
    for d in (1, 2, 3):
        for mine, theirs, device in (
            (tb.at[c, pl.ds(0, 2), :, z], tb.at[c, pl.ds(0, 2), :, zs_[4 - d]], zdev[d]),
            (tb.at[c, pl.ds(2, 2), x], tb.at[c, pl.ds(2, 2), xs[4 - d]], xdev[d]),
        ):
            t3.append(rcopy(mine, mine, device, start=False))
            t_on.append(rcopy(theirs, theirs, sibling, start=False))

    def t3_start(core):
        @pl.when(c == core)
        def _():
            for cp in t3:
                cp.cp.start()

    def t3_forward(core):
        @pl.when(c == core)
        def _():
            for cp, on in zip(t3, t_on):
                cp.cp.wait_recv()
                on.cp.start()

    def t3_sibling(core):
        @pl.when(c == core)
        def _():
            for cp in sib_t + t_on:
                cp.cp.wait_recv()

    t3_start(0)
    sib_s = ([], [])
    for i in range(4):
        if i:
            s3[2 * i - 2].wait_recv()
        r = s_all.at[0, :, zs_[(4 - i) % 4], :, ccol]
        sib_s[0].append(rcopy(r, r, sibling))
    for i in range(4):
        if i:
            s3[2 * i - 1].wait_recv()
        r = s_all.at[1, xs[(4 - i) % 4], :, :, ccol]
        sib_s[1].append(rcopy(r, r, sibling))
    w_wait()

    z_cp = ([], [])
    for k in range(2):
        for cp in sib_s[k]:
            cp.wait_recv()
        rows = pl.ds(k * 256, 256)
        lhs = s_all[k].reshape(256, HS)
        for n in range(4):
            cols = pl.ds(n * 256, 256)
            zs[rows, cols] = encode(jnp.dot(lhs, ws[1, :, cols], preferred_element_type=jnp.float32))
            z_cp[k].append(rcopy(zs.at[rows, cols], zr.at[rows, cols], partner))
        if k == 1:
            t3_start(1)
    def own_logits(k):
        rows = pl.ds(k * 256, 256)

        @pl.loop(0, 4)
        def _(n):
            cols = pl.ds(pl.multiple_of(n * 256, 256), 256)
            zo[rows, cols] = jnp.dot(s_all[k].reshape(256, HS), ws[0, :, cols], preferred_element_type=jnp.float32)

    own_logits(0)
    t3_forward(0)
    own_logits(1)
    t3_sibling(1)
    o = lax.broadcasted_iota(jnp.int32, (256, 256), 0)
    src = lax.broadcasted_iota(jnp.int32, (256, 256), 1)
    o_j, o_r = o // 64, lax.rem(o, 4)
    o_h, o_z = lax.rem(o // 32, 2), lax.rem(o // 16, 2) * 2 + lax.rem(o // 4, 2)
    o_x = lax.rem(o // 8, 2)
    perm = (src == o_h * 128 + o_x * 64 + o_z * 16 + o_j * 4 + o_r).astype(jnp.bfloat16)

    def permute(k):
        @pl.loop(4 * k, 4 * k + 4)
        def _(g):
            c_, p_, x_ = g // 4, lax.rem(g // 2, 2), lax.rem(g, 2)
            pieces = [tb[c_, 2 * a + p_, 2 * x_ + b].reshape(64, KT) for a in range(2) for b in range(2)]
            out = jnp.dot(perm, jnp.concatenate(pieces, axis=0), preferred_element_type=jnp.float32)
            out = out.astype(jnp.bfloat16)
            for j in range(4):
                tn[pl.ds(pl.multiple_of(g * 64, 64), 64), j * KT : (j + 1) * KT] = out[j * 64 : (j + 1) * 64]

    def teacher(k):
        rows = pl.ds(k * 256, 256)

        @pl.loop(0, 4)
        def _(n):
            cols = pl.ds(pl.multiple_of(n * 256, 256), 256)
            logits = jnp.dot(tn[rows, :], wt[:, cols], preferred_element_type=jnp.float32)
            et[rows, cols] = jnp.exp(CAP * jnp.tanh(logits / CAP))

    permute(0)
    teacher(0)
    t3_forward(1)
    tw_cp.wait_recv()
    w_nat = [[column(tw2[i, b, 0:1, :]) for b in range(2)] for i in range(2)]
    g_cp = {}
    gcol = pl.ds(pl.multiple_of(p * VT, VT), VT)
    ocol = pl.ds(pl.multiple_of((1 - p) * VT, VT), VT)

    def g_send(k, i):
        region = g_all.at[pl.ds(k * 256 + i * 128, 128), gcol]
        g_cp[k, i] = rcopy(region, region, partner)

    me_xz = x * 4 + z

    def exps(k):
        for cp in z_cp[k]:
            cp.wait_recv()
        for i in range(2):
            rows = pl.ds(k * 256 + i * 128, 128)

            @pl.loop(0, 8)
            def _(n):
                cols = pl.ds(pl.multiple_of(n * 128, 128), 128)
                z_ = zo[rows, cols] + decode(zr[rows, cols])
                zp[rows, cols] = z_
                th_ = jnp.tanh(z_ / CAP)
                zo[rows, cols] = jnp.exp(CAP * th_)
                slope[rows, cols] = 1.0 - th_ * th_

            ar_s[k, i : i + 1, :] = row_sums(zo[rows, :])
            ar_s[k, 2 + i : 3 + i, :] = row_sums(et[rows, :])
        ar_s[k, 4:8, :] = jnp.zeros((4, 128), jnp.float32)
        return rcopy(ar_s.at[k], ar_c.at[k], sibling)

    def to_plane(k, cp):
        cp.wait_recv()
        ar_r[k, me_xz] = ar_s[k] + ar_c[k]
        mine = ar_r.at[k, me_xz]
        return [rcopy(mine, mine, dev(p, xs[a], c, h, zs_[b])) for a, b in plane[1:]]

    def to_column(k, cps):
        for cp in cps:
            cp.wait_recv()
        ar_y[k, y] = jnp.sum(ar_r[k], axis=0)
        mine = ar_y.at[k, y]
        return [rcopy(mine, mine, ydev[d]) for d in (1, 2, 3)]

    def total(k, cps):
        for cp in cps:
            cp.wait_recv()
        return jnp.sum(ar_y[k], axis=0)

    def grads(k, i, totals):
        rows = pl.ds(k * 256 + i * 128, 128)
        w_col = jnp.concatenate(
            [
                w_nat[i][b7][b6 * 64 + k * 32 + b43 * 8 :][:8]
                for b7 in range(2)
                for b43 in range(4)
                for b6 in range(2)
            ],
            axis=0,
        )
        s_col = 1.0 / column(totals[i : i + 1, :])
        t_col = 1.0 / column(totals[2 + i : 3 + i, :])

        @pl.loop(0, 8)
        def _(n):
            cols = pl.ds(pl.multiple_of(n * 128, 128), 128)
            probs = (et[rows, cols] * t_col).astype(jnp.bfloat16).astype(jnp.float32)
            grad = w_col * (zo[rows, cols] * s_col - probs) * slope[rows, cols]
            g_all[rows, pl.ds(pl.multiple_of(p * VT + n * 128, 128), 128)] = grad.astype(jnp.bfloat16)

    nt = (((1,), (1,)), ((), ()))

    def own_grad(k):
        rows = pl.ds(k * 256, 256)

        @pl.loop(0, 7)
        def _(n):
            w_rows = pl.ds(pl.multiple_of(n * 256, 256), 256)
            dacc[rows, w_rows] = lax.dot_general(
                g_all[rows, gcol], ws[0, w_rows, :], nt, preferred_element_type=jnp.float32
            )

    sib0 = exps(0)
    plane0 = to_plane(0, sib0)
    t3_sibling(0)
    for cp in sib_t + t3 + t_on:
        cp.here = True
    permute(1)
    column0 = to_column(0, plane0)
    teacher(1)
    sib1 = exps(1)
    totals = total(0, column0)
    grads(0, 0, totals)
    g_send(0, 0)
    plane1 = to_plane(1, sib1)
    grads(0, 1, totals)
    column1 = to_column(1, plane1)
    g_send(0, 1)
    own_grad(0)
    totals = total(1, column1)
    for i in range(2):
        grads(1, i, totals)
        g_send(1, i)

    for k in range(2):
        for i in range(2):
            rows = pl.ds(k * 256 + i * 128, 128)
            n = 2 * k + i
            aq_s[n : n + 1, :] = row_sums(g_all[rows, gcol].astype(jnp.float32) * zp[rows, :])
    aq_s[4:8, :] = jnp.zeros((4, 128), jnp.float32)
    q_sib = rcopy(aq_s, aq_c, sibling)
    own_grad(1)
    q_sib.wait_recv()
    aq_r[me_xz] = aq_s[...] + aq_c[...]
    mine = aq_r.at[me_xz]
    q_plane = [rcopy(mine, mine, dev(p, xs[a], c, h, zs_[b])) for a, b in plane[1:]]
    rs_sem = counter[0]
    counter[0] += 4
    slot = x * 4 + z
    xcol = pl.ds(pl.multiple_of((1 - c) * CS, 128), CS)

    def rs_send(k, i, a, b):
        x_ = 2 * i + lax.rem(x + a, 2)
        return pltpu.make_async_remote_copy(
            src_ref=rs_s.at[k, x_, zs_[b]], dst_ref=rs_r.at[k, slot],
            send_sem=ssem.at[rs_sem + k], recv_sem=rsem.at[rs_sem + k],
            device_id=dev(p, x_, c, h, zs_[b]), device_id_type=MESH,
        )

    pieces = [(a, b) for b in range(4) for a in range(2)]

    def scatter(k, first, size):
        rows = pl.ds(k * 256 + first, size)

        @pl.loop(0, 7)
        def _(n):
            w_rows = pl.ds(pl.multiple_of(n * 256, 256), 256)
            dacc[rows, w_rows] += lax.dot_general(
                g_all[rows, ocol], ws[1, w_rows, :], nt, preferred_element_type=jnp.float32
            )

        rsib_s[rows, :] = dacc[rows, xcol].astype(jnp.bfloat16)
        return rcopy(rsib_s.at[rows], rsib_r.at[rows], sibling)

    def tiles_out(k, first, size, cp):
        rows = pl.ds(k * 256 + first, size)
        cp.wait_recv()
        both = (dacc[rows, ccol] + rsib_r[rows, :].astype(jnp.float32)).astype(jnp.bfloat16)
        rs_s[k, first // 64 : (first + size) // 64] = both.reshape(size // 64, 4, 16, CS)
        for i in range(first // 128, (first + size) // 128):
            for a, b in pieces[1:]:
                rs_send(k, i, a, b).start()

            @pl.when(x // 2 != i)
            def _():
                rs_send(k, i, 0, 0).start()

            def rs_end(i=i):
                for a, b in pieces[1:]:
                    rs_send(k, i, a, b).wait_send()

                @pl.when(x // 2 != i)
                def _():
                    rs_send(k, i, 0, 0).wait_send()

            ends.append(rs_end)

    def gather_sum(k):
        rwait(rs_r.at[k, pl.ds(0, 15)], rsem.at[rs_sem + k])
        rs_r[k, slot] = rs_s[k, x, z]
        fin_s[k] = jnp.sum(rs_r[k].astype(jnp.float32), axis=0)
        own = fin_s.at[k, pl.ds(pl.multiple_of(c * 8, 8), 8)]
        other = fin_s.at[k, pl.ds(pl.multiple_of((1 - c) * 8, 8), 8)]

        def f_copy(n, src, device):
            return pltpu.make_async_remote_copy(
                src_ref=src, dst_ref=fin.at[c, h], send_sem=ssem.at[fin_sem + n], recv_sem=rsem.at[fin_sem + n],
                device_id=device, device_id_type=MESH,
            )

        @pl.when(h == k)
        def _():
            fin[c, h] = own[...]
            f_copy(0, other, sibling).start()

        @pl.when(h != k)
        def _():
            f_copy(1, own, hdev).start()
            f_copy(2, other, cross).start()

        def f_end():
            @pl.when(h == k)
            def _():
                f_copy(0, other, sibling).wait_send()

            @pl.when(h != k)
            def _():
                f_copy(1, own, hdev).wait_send()
                f_copy(2, other, cross).wait_send()

        ends.append(f_end)

    fin_sem = counter[0]
    counter[0] += 3
    g_cp[0, 0].wait_recv()
    g_cp[0, 1].wait_recv()
    part = scatter(0, 0, 256)

    g_cp[1, 0].wait_recv()
    tiles_out(0, 0, 256, part)
    part = scatter(1, 0, 128)
    for cp in q_plane:
        cp.wait_recv()
    aq_y[y] = jnp.sum(aq_r[...], axis=0)
    mine = aq_y.at[y]
    q_column = [rcopy(mine, mine, ydev[d]) for d in (1, 2, 3)]
    g_cp[1, 1].wait_recv()
    tiles_out(1, 0, 128, part)
    part = scatter(1, 128, 128)
    tiles_out(1, 128, 128, part)
    for k in range(2):
        for j in range(7):
            cols = pl.ds(j * 256, 256)
            st[j * 256 : (j + 1) * 256, k * 256 : (k + 1) * 256] = s_all[k, :, :, :, cols].reshape(256, 256).T
    st_cp = pltpu.make_async_copy(st, st_out, lsem.at[3])
    st_cp.start()
    ends.append(st_cp.wait)
    @pl.loop(0, 7)
    def _(n):
        rows = pl.ds(pl.multiple_of(n * 256, 256), 256)
        wt[rows, :] = jnp.dot(st[rows, :], g_all[:, gcol], preferred_element_type=jnp.float32).astype(jnp.bfloat16)

    dw_cp = pltpu.make_async_copy(wt.at[pl.ds(0, HS)], dw_own, lsem.at[5])
    dw_cp.start()
    ends.append(dw_cp.wait)
    gather_sum(0)
    g_out_cp = pltpu.make_async_copy(g_all.at[:, ocol], g_out, lsem.at[4])
    g_out_cp.start()
    ends.append(g_out_cp.wait)
    for cp in q_column:
        cp.wait_recv()
    q_sum[...] = jnp.sum(aq_y[...], axis=0)
    q_col[...] = column(q_sum[pl.ds(2 * h + x // 2, 1), :])
    q = q_col[pl.ds(pl.multiple_of(lax.rem(x, 2) * 64 + z * 16 + c * 8, 8), 8), :][:, :1]
    gather_sum(1)
    for n in range(3):
        rwait(fin.at[0, 0], rsem.at[fin_sem + n])
    scaled = jnp.concatenate([fin[0, 0] + fin[0, 1], fin[1, 0] + fin[1, 1]], axis=-1) * gain
    dh_out[...] = stud_r * scaled - sx * (stud_r * stud_r) * q / DS

    finish()


def head(th, tg, sh, sg, tw, wt, ws):
    f32, bf16 = jnp.float32, jnp.bfloat16
    vmem = pl.BlockSpec(memory_space=pltpu.VMEM)
    hbm = pl.BlockSpec(memory_space=pl.ANY)
    scratch = [
        pltpu.VMEM((DT, VT), bf16),
        pltpu.VMEM((2, HS, VT), bf16),
        pltpu.VMEM((16, KT), f32),
        pltpu.VMEM((2, 4, 4, 4, 16, KT), bf16),
        pltpu.VMEM((512, DT), bf16),
        pltpu.VMEM((2, 2, 2, 8, 128), f32),
        pltpu.VMEM((2, 8, CS), f32),
        pltpu.VMEM((2, 16, CS), f32),
        pltpu.VMEM((2, 4, 4, 16, HS), bf16),
        pltpu.VMEM((HS, 512), bf16),
        pltpu.VMEM((512, VT), bf16),
        pltpu.VMEM((512, VT), bf16),
        pltpu.VMEM((512, VT), f32),
        pltpu.VMEM((512, VT), f32),
        pltpu.VMEM((512, VT), f32),
        pltpu.VMEM((512, 2 * VT), bf16),
        pltpu.VMEM((2, 2, 8, 128), f32),
        pltpu.VMEM((2, 8, 128), f32),
        pltpu.VMEM((2, 8, 128), f32),
        pltpu.VMEM((2, 16, 8, 128), f32),
        pltpu.VMEM((2, 4, 8, 128), f32),
        pltpu.VMEM((512, HS), f32),
        pltpu.VMEM((512, CS), bf16),
        pltpu.VMEM((512, CS), bf16),
        pltpu.VMEM((2, 4, 4, 16, CS), bf16),
        pltpu.VMEM((2, 16, 16, CS), bf16),
        pltpu.VMEM((2, 16, CS), f32),
        pltpu.VMEM((2, 2, 8, CS), f32),
        pltpu.VMEM((512, VT), f32),
        pltpu.VMEM((8, 128), f32),
        pltpu.VMEM((8, 128), f32),
        pltpu.VMEM((16, 8, 128), f32),
        pltpu.VMEM((4, 8, 128), f32),
        pltpu.VMEM((8, 128), f32),
        pltpu.VMEM((128, 128), f32),
        pltpu.SemaphoreType.DMA((160,)),
        pltpu.SemaphoreType.DMA((160,)),
        pltpu.SemaphoreType.DMA((6,)),
    ]
    return pl.pallas_call(
        head_kernel,
        out_shape=(
            jax.ShapeDtypeStruct((8, HS), f32),
            jax.ShapeDtypeStruct((HS, 512), bf16),
            jax.ShapeDtypeStruct((512, VT), bf16),
            jax.ShapeDtypeStruct((HS, VT), bf16),
        ),
        in_specs=[vmem] * 5 + [hbm] * 2,
        out_specs=(vmem, hbm, hbm, hbm),
        scratch_shapes=scratch,
        compiler_params=pltpu.CompilerParams(
            collective_id=0, has_side_effects=True, vmem_limit_bytes=58 * 1024 * 1024
        ),
        name="head",
    )(th, tg, sh, sg, tw, wt, ws)


def weight_kernel(dh_ref, own_hbm, st_hbm, g_hbm, dh_out, dw_out, st, g, own, other, in_sem, out_sem):
    p = lax.axis_index("pair")
    blocks = [pl.ds(256 * i, 256) for i in range(7)]
    own_cols = pl.ds(pl.multiple_of(p * VT, VT), VT)
    other_cols = pl.ds(pl.multiple_of((1 - p) * VT, VT), VT)
    g_in = pltpu.make_async_copy(g_hbm, g, in_sem.at[0])
    st_in = [pltpu.make_async_copy(st_hbm.at[b], st.at[b], in_sem.at[1 + i]) for i, b in enumerate(blocks)]
    own_in = [pltpu.make_async_copy(own_hbm.at[b], own.at[b], in_sem.at[8 + i]) for i, b in enumerate(blocks)]
    for cp in [g_in, *st_in, *own_in]:
        cp.start()
    dh_out[...] = dh_ref[...]
    g_in.wait()
    done = []
    for i, b in enumerate(blocks):
        st_in[i].wait()
        other[b, :] = jnp.dot(st[b, :], g[...], preferred_element_type=jnp.float32).astype(jnp.bfloat16)
        done.append(pltpu.make_async_copy(other.at[b], dw_out.at[b, other_cols], out_sem.at[i]))
        done[-1].start()
        own_in[i].wait()
        done.append(pltpu.make_async_copy(own.at[b], dw_out.at[b, own_cols], out_sem.at[7 + i]))
        done[-1].start()
    for cp in done:
        cp.wait()


def finish_weight(d_hidden, own, st, g):
    vmem = pl.BlockSpec(memory_space=pltpu.VMEM)
    hbm = pl.BlockSpec(memory_space=pl.ANY)
    return pl.pallas_call(
        weight_kernel,
        out_shape=(
            jax.ShapeDtypeStruct((8, HS), jnp.float32),
            jax.ShapeDtypeStruct((HS, 2 * VT), jnp.bfloat16),
        ),
        in_specs=[vmem, hbm, hbm, hbm],
        out_specs=(vmem, hbm),
        scratch_shapes=[
            pltpu.VMEM((HS, 512), jnp.bfloat16),
            pltpu.VMEM((512, VT), jnp.bfloat16),
            pltpu.VMEM((HS, VT), jnp.bfloat16),
            pltpu.VMEM((HS, VT), jnp.bfloat16),
            pltpu.SemaphoreType.DMA((15,)),
            pltpu.SemaphoreType.DMA((14,)),
        ],
        compiler_params=pltpu.CompilerParams(vmem_limit_bytes=58 * 1024 * 1024),
        name="weight",
    )(d_hidden, own, st, g)


def per_device(
    teacher_hidden,
    teacher_gain,
    teacher_weight,
    student_hidden,
    student_gain,
    student_weight,
    token_weight,
):
    d_hidden, st, g, own = head(
        teacher_hidden,
        teacher_gain,
        student_hidden,
        student_gain,
        token_weight,
        teacher_weight.reshape(DT, VT),
        student_weight,
    )
    return finish_weight(d_hidden, own, st, g)


def solution(mesh):
    return jax.shard_map(
        per_device,
        mesh=mesh,
        in_specs=(
            P(("pair", "vocab", "tok"), None),
            P(),
            P(None, ("vocab", "tok"), "pair", None),
            P(("vocab", "tok"), "pair"),
            P("pair"),
            P("pair", ("vocab", "tok")),
            P("pair"),
        ),
        out_specs=(P(("vocab", "tok"), "pair"), P("pair", ("vocab", "tok"))),
        check_vma=False,
    )
```
